128 devices in a mesh: fsdp: 16 (over y, x_hi, core), seq: 8 (over x_lo, z).
Axes of the slice: x: 4 (x_hi: 2, x_lo: 2; x = x_hi * 2 + x_lo), y: 4, z: 4, core: 2. Of those that a mesh axis runs over, the one named last changes fastest.
Arguments:
- normed_input: bfloat16 [16, 2048, 3072], P('fsdp', 'seq'), may hold values from -6 to 6
- queries: bfloat16 [16, 2048, 3072], P('fsdp', 'seq'), may hold values from -96 to 96
- saved_keys: bfloat16 [16, 2048, 3072], P('fsdp', 'seq'), may hold values from -6 to 6
- saved_values: bfloat16 [16, 2048, 3072], P('fsdp', 'seq'), may hold values from -6 to 6
- attention_out: bfloat16 [16, 2048, 3072], P('fsdp', 'seq'), may hold values from -6 to 6
- output_grad: bfloat16 [16, 2048, 3072], P('fsdp', 'seq'), may hold values from -6 to 6
- output_weight: bfloat16 [3072, 3072], P('fsdp'), may hold values from -0.109375 to 0.109375
- gate_table: float32 [64, 3072], replicated, may hold values from 0.25 to 2
- timestep: int32 [16], P('fsdp'), may hold values from 0 to 63
- entry_factor: bfloat16 [3072, 64], replicated, may hold values from -0.109375 to 0.109375
- merged_factor: bfloat16 [9216, 128], replicated, may hold values from -1.5 to 1.5
- mixed_factor: bfloat16 [3072, 64], replicated, may hold values from -0.109375 to 0.109375
- result_factor: bfloat16 [3072, 128], replicated, may hold values from -0.109375 to 0.109375
Outputs:
- sketches: float32 [16, 2, 8192], P('fsdp', None, 'seq')
The draws below stay inside these ranges and needn't reach their ends.
All inputs are finite; a program needn't handle non-finite values.
Results may differ from the reference program's by a relative error of at most 0.0056.
Values may be sent and summed in bfloat16 or wider, within the bound.
A program may use at most 128 MiB of HBM per device.

```python
import math
import jax
import jax.numpy as jnp
from jax import lax

HEADS = 24
HD = 128
D = 3072
SEQ = 2048
IMAGES = 16
STEPS = 64
RANK_IN = 64
RANK_OUT = 128


def drawn_picks(key):
    key_base = jax.random.truncated_normal(jax.random.fold_in(key, 101), -6.0, 6.0, (IMAGES, SEQ, D), jnp.float32)
    return key_base


def draw_saved_keys(key, part):
    key_base = drawn_picks(key)
    return key_base.astype(jnp.bfloat16)


def draw_queries(key, part):
    key = jax.random.fold_in(key, 7)
    drawn = jax.random.truncated_normal(key, -6.0, 6.0, (IMAGES, SEQ, D), jnp.float32)
    return drawn.astype(jnp.bfloat16)


def touch_ends(result, rng, least, largest):
    shape = result.shape
    place = [jax.random.randint(jax.random.fold_in(rng, axis), (), 0, shape[axis]) for axis in range(len(shape))]
    result = result.at[tuple(place)].set(least)
    longest = shape.index(max(shape))
    place[longest] = (place[longest] + 1) % shape[longest]
    return result.at[tuple(place)].set(largest)


def levels(rng, shape, shards, low, top_value):
    loudness, own = 1.0, jax.random.fold_in(rng, 6)
    for axis_at, blocks in shards:
        draws = jnp.exp(jax.random.uniform(jax.random.fold_in(own, axis_at), (blocks,), jnp.float32, low / len(shards), top_value / len(shards)))
        loudness = loudness * jnp.repeat(draws, shape[axis_at] // blocks).reshape([-1 if axis == axis_at else 1 for axis in range(len(shape))])
    return loudness


def scatter_about(rng, dims, deviation, bound, shards=(), held_as=jnp.bfloat16):
    gain = levels(rng, dims, shards, -0.22, 0.18) if shards else 1.0
    values = jax.random.normal(rng, dims, jnp.float32) * deviation * gain
    return jnp.minimum(jnp.maximum(values, -bound), bound).astype(held_as)


def setup_inputs(seed: int = 0) -> dict:
    streams_of = jax.random.split(jax.random.key(seed), 14)
    normed_input = scatter_about(streams_of[0], (IMAGES, SEQ, D), 1.0, 6.0, ((0, 16), (1, 8)))
    queries = draw_queries(jax.random.fold_in(streams_of[13], 71), 0)
    saved_keys = draw_saved_keys(jax.random.fold_in(streams_of[13], 71), 0)
    saved_values = scatter_about(streams_of[3], (IMAGES, SEQ, D), 1.0, 6.0, ((0, 16), (1, 8)))
    attention_out = scatter_about(streams_of[4], (IMAGES, SEQ, D), 1.0, 6.0, ((0, 16), (1, 8)))
    output_grad = scatter_about(streams_of[5], (IMAGES, SEQ, D), 1.0, 6.0, ((0, 16), (1, 8)))
    output_weight = scatter_about(streams_of[6], (D, D), D ** -0.5, 0.109375, ((0, 16),))
    gate_table = jnp.clip(jax.random.uniform(streams_of[7], (STEPS, D), jnp.float32, 0.25, 2.0), 0.25, 2.0)
    timestep = touch_ends(jax.random.randint(streams_of[8], (IMAGES,), 0, STEPS), jax.random.fold_in(streams_of[8], 1), 0, STEPS - 1).astype(jnp.int32)
    entry_factor = scatter_about(streams_of[9], (D, RANK_IN), D ** -0.5, 0.109375)
    merged_factor = scatter_about(streams_of[10], (3 * D, RANK_OUT), 0.25, 1.5)
    mixed_factor = scatter_about(streams_of[11], (D, RANK_IN), D ** -0.5, 0.109375)
    result_factor = scatter_about(streams_of[12], (D, RANK_OUT), D ** -0.5, 0.109375)
    return {"normed_input": normed_input, "queries": queries, "saved_keys": saved_keys, "saved_values": saved_values, "attention_out": attention_out, "output_grad": output_grad, "output_weight": output_weight, "gate_table": gate_table, "timestep": timestep, "entry_factor": entry_factor, "merged_factor": merged_factor, "mixed_factor": mixed_factor, "result_factor": result_factor}


def matmul(left, right):
    return jnp.dot(left.astype(jnp.float32), right.astype(jnp.float32), precision=lax.Precision.HIGHEST)

def head_backward(query_head, key_head, value_head, grad_head):
    score_scale = 1.0 / math.sqrt(HD)
    scores = matmul(query_head, key_head.T) * score_scale
    row_max = lax.optimization_barrier(jnp.max(scores, axis=-1, keepdims=True))
    shifted = jnp.exp(scores - row_max)
    weights = shifted / lax.optimization_barrier(jnp.sum(shifted, axis=-1, keepdims=True))
    rounded = weights.astype(jnp.bfloat16)
    value_grad = matmul(rounded.T, grad_head).astype(jnp.bfloat16)
    weight_grad = matmul(grad_head, value_head.T)
    centre = lax.optimization_barrier(jnp.sum(weights * weight_grad, axis=-1, keepdims=True))
    score_grad = (weights * (weight_grad - centre) * score_scale).astype(jnp.bfloat16)
    query_grad = matmul(score_grad, key_head).astype(jnp.bfloat16)
    key_grad = matmul(score_grad.T, query_head).astype(jnp.bfloat16)
    return (query_grad, key_grad, value_grad)

def split_heads(values):
    return values.reshape(SEQ, HEADS, HD).transpose(1, 0, 2)

def join_heads(values):
    return values.transpose(1, 0, 2).reshape(SEQ, D)

def reference(normed_input, queries, saved_keys, saved_values, attention_out, output_grad, output_weight, gate_table, timestep, entry_factor, merged_factor, mixed_factor, result_factor):
    norm_factor = 1.0 / math.sqrt(SEQ)

    def one_image(inputs):
        normed, query_all, key_all, value_all, attended, grad_out, step_index = inputs
        gate_row = gate_table[step_index]
        scaled_grad = (gate_row[None, :] * grad_out.astype(jnp.float32)).astype(jnp.bfloat16)
        attention_grad = matmul(scaled_grad, output_weight.T).astype(jnp.bfloat16)
        head_grads = lax.map(lambda group: head_backward(group[0], group[1], group[2], group[3]), (split_heads(query_all), split_heads(key_all), split_heads(value_all), split_heads(attention_grad)))
        merged_grad = jnp.concatenate([join_heads(head_grads[0]), join_heads(head_grads[1]), join_heads(head_grads[2])], axis=1)
        entry_left = matmul(normed, entry_factor)
        merged_right = matmul(merged_grad, merged_factor)
        mixed_left = matmul(attended, mixed_factor)
        mixed_right = matmul(scaled_grad, result_factor)
        sketch_mixed = matmul(mixed_left.T, mixed_right) * norm_factor
        sketch_merged = matmul(entry_left.T, merged_right) * norm_factor
        return jnp.stack([sketch_mixed.reshape(-1), sketch_merged.reshape(-1)])
    return lax.map(one_image, (normed_input, queries, saved_keys, saved_values, attention_out, output_grad, timestep))
```

```python
import math

import jax
import jax.numpy as jnp
from jax import lax
from jax.experimental import pallas as pl
from jax.experimental.pallas import tpu as pltpu
from jax.sharding import PartitionSpec as P

F32 = jnp.float32
BF16 = jnp.bfloat16
MESH = pl.DeviceIdType.MESH

D = 3072
HD = 128
TOK = 256
SEQ = 2048
PEERS = 8
HPD = 3
RIN = 64
ROUT = 128
WROWS = 192
HALF = 96
RINGS = 4
SCALE = 1.0 / math.sqrt(HD)
EXP2_SCALE = SCALE * math.log2(math.e)
NORM = 1.0 / math.sqrt(SEQ)
QB = 512
KB = 256

NN = (((1,), (0,)), ((), ()))
NT = (((1,), (1,)), ((), ()))
TN = (((0,), (0,)), ((), ()))


def dot(left, right, dims=NN, precision=None):
    return lax.dot_general(left, right, dims, precision=precision, preferred_element_type=F32)


def split(values):
    high = values.astype(BF16)
    return high, (values - high.astype(F32)).astype(BF16)


def dot_split(values, right, dims=NN):
    high, low = split(values)
    return dot(high, right, dims) + dot(low, right, dims)


def fold(values, reduce):
    rows, columns = values.shape
    return reduce(values.reshape(rows // 8, 8, columns), axis=0)


def attend_block(start, first, head, qb, kb_ref, vb, gt, et, s_ref, p_ref, dp_ref, accv, acck):
    q_rows = pl.ds(start, QB)
    qf = qb[head, q_rows, :].astype(F32).T
    q_both = jnp.concatenate(split(qf * EXP2_SCALE), 0)
    steps = SEQ // KB
    top = None
    for step in range(steps):
        rows = pl.ds(step * KB, KB)
        keys = kb_ref[head, rows, :]
        scores = dot(jnp.concatenate([keys, keys], 1), q_both)
        s_ref[rows, :] = scores
        part = fold(scores, jnp.max)
        top = part if top is None else jnp.maximum(top, part)
    top = jnp.max(top, axis=0, keepdims=True)
    grads = gt[pl.ds(pl.multiple_of(head * HD, HD), HD), q_rows]
    total, centre = None, None
    for step in range(steps):
        rows = pl.ds(step * KB, KB)
        probs = jnp.exp2(s_ref[rows, :] - top)
        prob_grad = dot(vb[head, rows, :], grads)
        part_total = fold(probs, jnp.sum)
        part_centre = fold(probs * prob_grad, jnp.sum)
        total = part_total if total is None else total + part_total
        centre = part_centre if centre is None else centre + part_centre
        p_ref[rows, :] = probs.astype(BF16)
        dp_ref[rows, :] = prob_grad
    inverse = 1.0 / jnp.sum(total, axis=0, keepdims=True)
    centre = jnp.sum(centre, axis=0, keepdims=True) * inverse
    grads_scaled = (grads.astype(F32) * inverse).astype(BF16)
    inverse = inverse * SCALE
    entry_high, entry_low = split(et[:, q_rows] * inverse)
    q_entry = jnp.concatenate([(qf * inverse).astype(BF16), entry_high, entry_low], 0)
    for step in range(steps):
        rows = pl.ds(step * KB, KB)
        probs = p_ref[rows, :]
        score_grad = (probs.astype(F32) * (dp_ref[rows, :] - centre)).astype(BF16)
        add_v = dot(probs, grads_scaled, NT)
        add_k = dot(score_grad, q_entry, NT)
        if first:
            accv[rows, :] = add_v
            acck[rows, :] = add_k
        else:
            accv[rows, :] += add_v
            acck[rows, :] += add_k


def kernel(
    xn, qh, kh, vh, ao, og, wh, gates, step_ref, ef, mergedf, mixf, resf,
    out,
    qb, kb_ref, vb, gt, et, sg, wb, gst, xv, av, gv, efv, mfv, rfv, fv,
    s_ref, p_ref, dp_ref, accv, acck, part, gather,
    load_sem, qkv_recv, qkv_send, w_recv, w_send, sg_recv, sg_send,
    g_recv, g_send, e_recv, e_send, r_recv, r_send,
):
    f = lax.axis_index("fsdp")
    s = lax.axis_index("seq")
    y = f // 4
    hi = (f // 2) % 2
    core = f % 2
    lo = s // 4
    zz = s % 4
    s_across = (1 - lo) * 4 + zz
    mate = (f + 1 - 2 * core, s)
    across_f = y * 4 + (1 - hi) * 2 + core
    across = (across_f, s_across)
    up = ((f + 4) % 16, s)
    down = ((f + 12) % 16, s)

    barrier = pltpu.get_barrier_semaphore()

    @pl.loop(1, 32)
    def _(step):
        target = (y * 4 + (f % 4 + step // 8) % 4, (s + step) % 8)
        pl.semaphore_signal(barrier, inc=1, device_id=target, device_id_type=MESH)

    for target in (up, down):
        pl.semaphore_signal(barrier, inc=1, device_id=target, device_id_type=MESH)

    loads = []

    def load(source, target):
        copy = pltpu.make_async_copy(source, target, load_sem.at[len(loads)])
        copy.start()
        loads.append(copy)
        return copy

    load_og = load(og.at[0], sg.at[0])
    load_gate = load(gates, gv)
    load_w = load(wh, wb.at[y])
    load_xn = load(xn.at[0], xv)
    load_ef = load(ef, efv)
    load_ao = load(ao.at[0], av)
    load_mf = load(mixf, mfv)
    load_rf = load(resf, rfv)
    load_f = [
        load(mergedf.at[pl.ds(pl.multiple_of(kind * D + s * 384, 128), 384), :], fv.at[kind])
        for kind in range(3)
    ]

    sources = (qh, kh, vh)
    targets = (qb, kb_ref, vb)
    here = pl.ds(pl.multiple_of(s * TOK, TOK), TOK)
    for head in range(HPD):
        for which in range(3):
            columns = pl.ds(pl.multiple_of(s * 384 + head * HD, HD), HD)
            pltpu.make_async_copy(
                sources[which].at[0, :, columns],
                targets[which].at[head, here, :],
                qkv_recv.at[which, head],
            ).start()

    load_og.wait()
    load_gate.wait()
    gate = gv[pl.ds(step_ref[0], 1), :]
    for row in range(0, TOK, 32):
        rows = pl.ds(row, 32)
        sg[0, rows, :] = (gate * sg[0, rows, :].astype(F32)).astype(BF16)

    pl.semaphore_wait(barrier, 33)

    def remote(source, target, send, recv, device):
        return pltpu.make_async_remote_copy(
            src_ref=source, dst_ref=target, send_sem=send, recv_sem=recv,
            device_id=device, device_id_type=MESH,
        )

    first_half = pl.ds(0, HALF)
    second_half = pl.ds(HALF, HALF)
    w_copies = [
        remote(wh.at[first_half], wb.at[y, first_half], w_send.at[0], w_recv.at[0], up),
        remote(wh.at[second_half], wb.at[y, second_half], w_send.at[1], w_recv.at[1], down),
        remote(wh.at[second_half], wb.at[y, second_half], w_send.at[2], w_recv.at[2], up),
        remote(wh.at[first_half], wb.at[y, first_half], w_send.at[3], w_recv.at[3], down),
    ]
    for copy in w_copies:
        copy.start()
    sg_across = remote(sg.at[0], sg.at[2], sg_send.at[1], sg_recv.at[1], across)
    sg_across.start()
    sg_mate = remote(sg.at[0], sg.at[1], sg_send.at[0], sg_recv.at[0], mate)
    sg_mate.start()

    for head in range(HPD):

        @pl.loop(1, PEERS)
        def _(step):
            peer = (s + step) % PEERS
            columns = pl.ds(pl.multiple_of(peer * 384 + head * HD, HD), HD)
            for which in range(3):
                remote(
                    sources[which].at[0, :, columns],
                    targets[which].at[head, here, :],
                    qkv_send.at[which, head],
                    qkv_recv.at[which, head],
                    (f, peer),
                ).start()

    load_xn.wait()
    load_ef.wait()
    entry = dot(xv[...], efv[...])
    et[:, here] = jnp.concatenate([entry, entry], 1).T[:RIN]

    @pl.loop(1, PEERS)
    def _(step):
        peer = (s + step) % PEERS
        remote(et.at[:, here], et.at[:, here], e_send, e_recv, (f, peer)).start()

    load_ao.wait()
    load_mf.wait()
    load_rf.wait()
    mixed_left = dot(av[...], mfv[...])
    mixed_left = jnp.concatenate([mixed_left, mixed_left], 1).T[:RIN]
    mixed_right = dot(sg[0], rfv[...])
    part[0] = dot(mixed_left, mixed_right, precision=lax.Precision.HIGHEST) * NORM

    def g_copies(chunk, image):
        token_block = s if image < 2 else s_across
        image_f = (f, mate[0], across_f, across_f + 1 - 2 * core)[image]
        peer = 2 * chunk + hi
        columns = pl.ds(pl.multiple_of(token_block * TOK, TOK), TOK)
        target = gt.at[pl.ds(pl.multiple_of(core * WROWS, WROWS), WROWS), columns]
        slot = chunk * 4 + image
        far = remote(
            gst.at[chunk, image], target, g_send.at[slot], g_recv, (image_f, peer)
        )
        near = pltpu.make_async_copy(gst.at[chunk, image], target, g_recv)
        return far, near, peer

    def make_g(chunk, image):
        gst[chunk, image] = dot(wb[chunk], sg[image], NT).astype(BF16)
        far, near, peer = g_copies(chunk, image)
        if image == 0:

            @pl.when(peer == s)
            def _():
                near.start()

            @pl.when(peer != s)
            def _():
                far.start()
        else:
            far.start()

    below, above, opposite = (y + 3) % 4, (y + 1) % 4, (y + 2) % 4
    load_w.wait()
    make_g(y, 0)
    sg_mate.wait_recv()
    make_g(y, 1)
    w_copies[0].wait_recv()
    relay_up = remote(
        wb.at[below, first_half], wb.at[below, first_half], w_send.at[4], w_recv.at[4], up
    )
    relay_up.start()
    w_copies[1].wait_recv()
    relay_down = remote(
        wb.at[above, second_half], wb.at[above, second_half], w_send.at[5], w_recv.at[5], down
    )
    relay_down.start()
    w_copies[2].wait_recv()
    w_copies[3].wait_recv()

    def two(image):
        @pl.loop(0, 2)
        def _(step):
            make_g((y + 1 + 2 * step) % 4, image)

    def four(image):
        @pl.loop(0, 4)
        def _(step):
            make_g((y + step) % 4, image)

    two(0)
    two(1)
    sg_across.wait_recv()
    sg_pass = remote(sg.at[2], sg.at[3], sg_send.at[2], sg_recv.at[2], mate)
    sg_pass.start()
    relay_up.wait_recv()
    relay_down.wait_recv()
    make_g(opposite, 0)
    make_g(opposite, 1)
    four(2)
    sg_pass.wait_recv()
    four(3)

    for copy in load_f:
        copy.wait()
    rest = pl.ds(0, SEQ - TOK)
    pltpu.make_async_copy(et.at[:, rest], et.at[:, rest], e_recv).wait()
    pltpu.make_async_copy(gt, gt, g_recv).wait()
    part[1] = jnp.zeros((RIN, ROUT), F32)

    @pl.loop(0, HPD)
    def _(head):
        for which in range(3):
            whole = targets[which].at[head]
            pltpu.make_async_copy(whole, whole, qkv_recv.at[which, head]).wait()
        refs = (qb, kb_ref, vb, gt, et, s_ref, p_ref, dp_ref, accv, acck)
        attend_block(0, True, head, *refs)

        @pl.loop(1, SEQ // QB)
        def _(block):
            attend_block(pl.multiple_of(block * QB, QB), False, head, *refs)

        entry_both = jnp.concatenate(split(et[...]), 0)
        value_part = dot(entry_both, accv[...].astype(BF16))
        key_part = dot(entry_both, acck[:, :HD].astype(BF16))
        query_part = dot_split(acck[:, HD:], kb_ref[head], TN)
        columns = pl.ds(pl.multiple_of(head * HD, HD), HD)
        sketch = None
        for kind, piece in enumerate((query_part, key_part, value_part)):
            term = dot_split(piece[:RIN] + piece[RIN:], fv[kind, columns, :])
            sketch = term if sketch is None else sketch + term
        part[1] += sketch * NORM

    @pl.loop(1, PEERS)
    def _(step):
        peer = (s + step) % PEERS
        rows = pl.ds(pl.multiple_of(peer * 8, 8), 8)
        remote(part.at[:, rows, :], gather.at[s], r_send, r_recv, (f, peer)).start()

    gather[s] = part[:, pl.ds(pl.multiple_of(s * 8, 8), 8), :]
    seven = gather.at[pl.ds(0, PEERS - 1)]
    pltpu.make_async_copy(seven, seven, r_recv).wait()
    summed = jnp.sum(gather[...], axis=0)
    for sketch in range(2):
        for row in range(8):
            out[0, sketch : sketch + 1, row * 128 : (row + 1) * 128] = summed[
                sketch, row : row + 1, :
            ]

    pltpu.make_async_copy(seven, seven, r_send).wait()
    pltpu.make_async_copy(et.at[:, rest], et.at[:, rest], e_send).wait()
    for head in range(HPD):
        for which in range(3):
            sent = targets[which].at[head, rest]
            pltpu.make_async_copy(sent, sent, qkv_send.at[which, head]).wait()
    for copy in w_copies + [relay_up, relay_down]:
        copy.wait_send()
    for copy in (sg_mate, sg_across, sg_pass):
        copy.wait_send()
    for image in range(4):

        @pl.loop(0, RINGS)
        def _(chunk):
            far, _, peer = g_copies(chunk, image)
            if image == 0:

                @pl.when(peer != s)
                def _():
                    far.wait_send()
            else:
                far.wait_send()


def local(*operands):
    dma = pltpu.SemaphoreType.DMA
    any_spec = pl.BlockSpec(memory_space=pl.ANY)
    in_specs = [any_spec] * 13
    in_specs[8] = pl.BlockSpec(memory_space=pltpu.SMEM)
    return pl.pallas_call(
        kernel,
        out_shape=jax.ShapeDtypeStruct((1, 2, RIN * ROUT // PEERS), F32),
        in_specs=in_specs,
        out_specs=pl.BlockSpec(memory_space=pltpu.VMEM),
        scratch_shapes=[
            pltpu.VMEM((HPD, SEQ, HD), BF16),
            pltpu.VMEM((HPD, SEQ, HD), BF16),
            pltpu.VMEM((HPD, SEQ, HD), BF16),
            pltpu.VMEM((HPD * HD, SEQ), BF16),
            pltpu.VMEM((RIN, SEQ), F32),
            pltpu.VMEM((4, TOK, D), BF16),
            pltpu.VMEM((RINGS, WROWS, D), BF16),
            pltpu.VMEM((RINGS, 4, WROWS, TOK), BF16),
            pltpu.VMEM((TOK, D), BF16),
            pltpu.VMEM((TOK, D), BF16),
            pltpu.VMEM((64, D), F32),
            pltpu.VMEM((D, RIN), BF16),
            pltpu.VMEM((D, RIN), BF16),
            pltpu.VMEM((D, ROUT), BF16),
            pltpu.VMEM((3, HPD * HD, ROUT), BF16),
            pltpu.VMEM((SEQ, QB), F32),
            pltpu.VMEM((SEQ, QB), BF16),
            pltpu.VMEM((SEQ, QB), F32),
            pltpu.VMEM((SEQ, HD), F32),
            pltpu.VMEM((SEQ, 2 * HD), F32),
            pltpu.VMEM((2, RIN, ROUT), F32),
            pltpu.VMEM((PEERS, 2, 8, ROUT), F32),
            dma((11,)),
            dma((3, HPD)),
            dma((3, HPD)),
            dma((6,)),
            dma((6,)),
            dma((3,)),
            dma((3,)),
            dma,
            dma((16,)),
            dma,
            dma,
            dma,
            dma,
        ],
        compiler_params=pltpu.CompilerParams(
            collective_id=0, has_side_effects=True, vmem_limit_bytes=60 << 20
        ),
        cost_estimate=pl.CostEstimate(
            flops=26 * 10**9, bytes_accessed=16 * 2**20, transcendentals=13 * 10**6
        ),
    )(*operands)


def solution(mesh):
    in_specs = (
        P("fsdp", "seq", None),
        P("fsdp", "seq", None),
        P("fsdp", "seq", None),
        P("fsdp", "seq", None),
        P("fsdp", "seq", None),
        P("fsdp", "seq", None),
        P("fsdp", None),
        P(),
        P("fsdp"),
        P(),
        P(),
        P(),
        P(),
    )
    out_specs = P("fsdp", None, "seq")
    return jax.shard_map(local, mesh=mesh, in_specs=in_specs, out_specs=out_specs, check_vma=False)
```

```python
import math

import jax
import jax.numpy as jnp
from jax import lax
from jax.experimental import pallas as pl
from jax.experimental.pallas import tpu as pltpu
from jax.sharding import PartitionSpec as P

F32 = jnp.float32
BF16 = jnp.bfloat16
MESH = pl.DeviceIdType.MESH

D = 3072
HD = 128
TOK = 256
SEQ = 2048
PEERS = 8
HPD = 3
RIN = 64
ROUT = 128
WROWS = 192
HALF = 96
RINGS = 4
SCALE = 1.0 / math.sqrt(HD)
EXP2_SCALE = SCALE * math.log2(math.e)
NORM = 1.0 / math.sqrt(SEQ)
SB = 256
GB = 1024
KB = 256
KEY_STEPS = SEQ // KB

NN = (((1,), (0,)), ((), ()))
NT = (((1,), (1,)), ((), ()))
TN = (((0,), (0,)), ((), ()))


def dot(left, right, dims=NN, precision=None):
    return lax.dot_general(left, right, dims, precision=precision, preferred_element_type=F32)


def split(values):
    high = values.astype(BF16)
    return high, (values - high.astype(F32)).astype(BF16)


def dot_split(values, right, dims=NN):
    high, low = split(values)
    return dot(high, right, dims) + dot(low, right, dims)


def fold(values, reduce):
    rows, columns = values.shape
    return reduce(values.reshape(rows // 8, 8, columns), axis=0)


def softmax_head(head, slot, qb, kb_ref, vb, s_ref, p_ref, l_ref, o_ref, vt):
    vt[...] = vb[head].T

    def queries(start):
        wide = qb[head, pl.ds(start, SB), :].astype(F32).T
        return jnp.concatenate(split(wide * EXP2_SCALE), 0)

    def score(both, side, step, top):
        rows = pl.ds(step * KB, KB)
        keys = kb_ref[head, rows, :]
        scores = dot(jnp.concatenate([keys, keys], 1), both)
        s_ref[side, rows, :] = scores
        part = fold(scores, jnp.max)
        return part if top is None else jnp.maximum(top, part)

    def exponential(columns, side, step, top, total, mixed):
        rows = pl.ds(step * KB, KB)
        probs = jnp.exp2(s_ref[side, rows, :] - top)
        part = fold(probs, jnp.sum)
        probs = probs.astype(BF16)
        p_ref[slot, rows, columns] = probs
        piece = dot(vt[:, rows], probs)
        if total is None:
            return part, piece
        return total + part, mixed + piece

    def finish(columns, total, mixed):
        l_ref[pl.ds(slot, 1), columns] = jnp.sum(total, axis=0, keepdims=True)
        o_ref[slot, :, columns] = mixed

    def highest(top):
        return jnp.max(top, axis=0, keepdims=True)

    def stage(block, side, top):
        columns = pl.ds(pl.multiple_of(block * SB, SB), SB)
        both = queries(pl.multiple_of((block + 1) * SB, SB))
        later, total, mixed = None, None, None
        for step in range(KEY_STEPS):
            later = score(both, 1 - side, step, later)
            total, mixed = exponential(columns, side, step, top, total, mixed)
        finish(columns, total, mixed)
        return highest(later)

    both, top = queries(0), None
    for step in range(KEY_STEPS):
        top = score(both, 0, step, top)
    blocks = SEQ // SB

    def pair(index, top):
        return stage(2 * index + 1, 1, stage(2 * index, 0, top))

    top = lax.fori_loop(0, blocks // 2 - 1, pair, highest(top))
    top = stage(blocks - 2, 0, top)
    columns = pl.ds(SEQ - SB, SB)
    total, mixed = None, None
    for step in range(KEY_STEPS):
        total, mixed = exponential(columns, 1, step, top, total, mixed)
    finish(columns, total, mixed)


def gradient_block(start, first, head, slot, qb, vb, gt, et, p_ref, l_ref, o_ref, accv, acck):
    columns = pl.ds(start, GB)
    inverse = 1.0 / l_ref[pl.ds(slot, 1), columns]
    grads = gt[pl.ds(pl.multiple_of(head * HD, HD), HD), columns]
    wide = grads.astype(F32)
    centre = jnp.sum(wide * o_ref[slot, :, columns], axis=0, keepdims=True) * inverse
    grads_scaled = (wide * inverse).astype(BF16)
    inverse = inverse * SCALE
    entry_high, entry_low = split(et[:, columns].astype(F32) * inverse)
    q_scaled = (qb[head, columns, :].astype(F32).T * inverse).astype(BF16)
    q_entry = jnp.concatenate([q_scaled, entry_high, entry_low], 0)
    for step in range(KEY_STEPS):
        rows = pl.ds(step * KB, KB)
        probs = p_ref[slot, rows, columns]
        prob_grad = dot(vb[head, rows, :], grads)
        score_grad = (probs.astype(F32) * (prob_grad - centre)).astype(BF16)
        add_v = dot(probs, grads_scaled, NT)
        add_k = dot(score_grad, q_entry, NT)
        if first:
            accv[rows, :] = add_v
            acck[rows, :] = add_k
        else:
            accv[rows, :] += add_v
            acck[rows, :] += add_k


def kernel(
    xn, qh, kh, vh, ao, og, wh, gates, step_ref, ef, mergedf, mixf, resf,
    out,
    qb, kb_ref, vb, gt, et, sg, wb, gst, xv, av, gv, efv, mfv, rfv, fv,
    s_ref, p_ref, l_ref, o_ref, vt, accv, acck, part, gather,
    load_sem, qkv_recv, qkv_send, w_recv, w_send, sg_recv, sg_send,
    g_recv, g_send, e_recv, e_send, r_recv, r_send,
):
    f = lax.axis_index("fsdp")
    s = lax.axis_index("seq")
    y = f // 4
    hi = (f // 2) % 2
    core = f % 2
    lo = s // 4
    zz = s % 4
    s_across = (1 - lo) * 4 + zz
    mate = (f + 1 - 2 * core, s)
    across_f = y * 4 + (1 - hi) * 2 + core
    across = (across_f, s_across)
    up = ((f + 4) % 16, s)
    down = ((f + 12) % 16, s)

    barrier = pltpu.get_barrier_semaphore()

    @pl.loop(1, 32)
    def _(step):
        target = (y * 4 + (f % 4 + step // 8) % 4, (s + step) % 8)
        pl.semaphore_signal(barrier, inc=1, device_id=target, device_id_type=MESH)

    for target in (up, down):
        pl.semaphore_signal(barrier, inc=1, device_id=target, device_id_type=MESH)

    loads = []

    def load(source, target):
        copy = pltpu.make_async_copy(source, target, load_sem.at[len(loads)])
        copy.start()
        loads.append(copy)
        return copy

    load_og = load(og.at[0], sg.at[0])
    load_gate = load(gates, gv)
    load_w = load(wh, wb.at[y])
    load_xn = load(xn.at[0], xv)
    load_ef = load(ef, efv)
    load_ao = load(ao.at[0], av)
    load_mf = load(mixf, mfv)
    load_rf = load(resf, rfv)
    load_f = [
        load(mergedf.at[pl.ds(pl.multiple_of(kind * D + s * 384, 128), 384), :], fv.at[kind])
        for kind in range(3)
    ]

    sources = (qh, kh, vh)
    targets = (qb, kb_ref, vb)
    here = pl.ds(pl.multiple_of(s * TOK, TOK), TOK)
    for head in range(HPD):
        for which in range(3):
            columns = pl.ds(pl.multiple_of(s * 384 + head * HD, HD), HD)
            pltpu.make_async_copy(
                sources[which].at[0, :, columns],
                targets[which].at[head, here, :],
                qkv_recv.at[which, head],
            ).start()

    pl.semaphore_wait(barrier, 33)

    def remote(source, target, send, recv, device):
        return pltpu.make_async_remote_copy(
            src_ref=source, dst_ref=target, send_sem=send, recv_sem=recv,
            device_id=device, device_id_type=MESH,
        )

    first_half = pl.ds(0, HALF)
    second_half = pl.ds(HALF, HALF)
    w_copies = [
        remote(wh.at[first_half], wb.at[y, first_half], w_send.at[0], w_recv.at[0], up),
        remote(wh.at[second_half], wb.at[y, second_half], w_send.at[1], w_recv.at[1], down),
        remote(wh.at[second_half], wb.at[y, second_half], w_send.at[2], w_recv.at[2], up),
        remote(wh.at[first_half], wb.at[y, first_half], w_send.at[3], w_recv.at[3], down),
    ]
    for copy in w_copies:
        copy.start()
    def peer_of(step):
        return ((lo + step // 4) % 2) * 4 + (zz + step) % 4

    def send_head(head):
        @pl.loop(1, PEERS)
        def _(step):
            peer = peer_of(step)
            columns = pl.ds(pl.multiple_of(peer * 384 + head * HD, HD), HD)
            for which in range(3):
                remote(
                    sources[which].at[0, :, columns],
                    targets[which].at[head, here, :],
                    qkv_send.at[which, head],
                    qkv_recv.at[which, head],
                    (f, peer),
                ).start()

    send_head(0)

    load_og.wait()
    load_gate.wait()
    gate = gv[pl.ds(step_ref[0], 1), :]
    for row in range(0, TOK, 32):
        rows = pl.ds(row, 32)
        sg[0, rows, :] = (gate * sg[0, rows, :].astype(F32)).astype(BF16)

    sg_across = remote(sg.at[0], sg.at[2], sg_send.at[1], sg_recv.at[1], across)
    sg_across.start()
    sg_mate = remote(sg.at[0], sg.at[1], sg_send.at[0], sg_recv.at[0], mate)
    sg_mate.start()

    send_head(1)

    load_xn.wait()
    load_ef.wait()
    et[:, here] = dot(efv[...], xv[...], NT).astype(BF16)

    @pl.loop(1, PEERS)
    def _(step):
        peer = peer_of(step)
        remote(et.at[:, here], et.at[:, here], e_send, e_recv, (f, peer)).start()

    load_ao.wait()
    load_mf.wait()
    load_rf.wait()
    mixed_left = dot(mfv[...], av[...], NT)
    mixed_right = dot(sg[0], rfv[...])
    part[0] = dot(mixed_left, mixed_right, precision=lax.Precision.HIGHEST) * NORM

    def g_copies(chunk, image):
        token_block = s if image < 2 else s_across
        image_f = (f, mate[0], across_f, across_f + 1 - 2 * core)[image]
        peer = 2 * chunk + hi
        columns = pl.ds(pl.multiple_of(token_block * TOK, TOK), TOK)
        target = gt.at[pl.ds(pl.multiple_of(core * WROWS, WROWS), WROWS), columns]
        slot = chunk * 4 + image
        far = remote(
            gst.at[chunk, image], target, g_send.at[slot], g_recv, (image_f, peer)
        )
        near = pltpu.make_async_copy(gst.at[chunk, image], target, g_recv)
        return far, near, peer

    def make_g(chunk, image):
        gst[chunk, image] = dot(wb[chunk], sg[image], NT).astype(BF16)
        far, near, peer = g_copies(chunk, image)
        if image == 0:

            @pl.when(peer == s)
            def _():
                near.start()

            @pl.when(peer != s)
            def _():
                far.start()
        else:
            far.start()

    below, above, opposite = (y + 3) % 4, (y + 1) % 4, (y + 2) % 4
    load_w.wait()
    make_g(y, 0)
    sg_mate.wait_recv()
    make_g(y, 1)
    w_copies[0].wait_recv()
    relay_up = remote(
        wb.at[below, first_half], wb.at[below, first_half], w_send.at[4], w_recv.at[4], up
    )
    relay_up.start()
    w_copies[1].wait_recv()
    relay_down = remote(
        wb.at[above, second_half], wb.at[above, second_half], w_send.at[5], w_recv.at[5], down
    )
    relay_down.start()

    def wait_head(head):
        for which in range(3):
            whole = targets[which].at[head]
            pltpu.make_async_copy(whole, whole, qkv_recv.at[which, head]).wait()

    def softmax_of(head, slot):
        softmax_head(head, slot, qb, kb_ref, vb, s_ref, p_ref, l_ref, o_ref, vt)

    wait_head(0)
    softmax_of(0, 0)
    w_copies[2].wait_recv()
    w_copies[3].wait_recv()

    def two(image):
        @pl.loop(0, 2)
        def _(step):
            make_g((y + 1 + 2 * step) % 4, image)

    def four(image):
        @pl.loop(0, 4)
        def _(step):
            make_g((y + step) % 4, image)

    two(0)
    two(1)
    sg_across.wait_recv()
    sg_pass = remote(sg.at[2], sg.at[3], sg_send.at[2], sg_recv.at[2], mate)
    sg_pass.start()
    make_g(y, 2)
    two(2)
    relay_up.wait_recv()
    relay_down.wait_recv()
    make_g(opposite, 0)
    make_g(opposite, 1)
    make_g(opposite, 2)
    sg_pass.wait_recv()
    four(3)
    send_head(2)
    wait_head(1)
    softmax_of(1, 1)

    for copy in load_f:
        copy.wait()
    rest = pl.ds(0, SEQ - TOK)
    pltpu.make_async_copy(et.at[:, rest], et.at[:, rest], e_recv).wait()
    pltpu.make_async_copy(gt, gt, g_recv).wait()
    part[1] = jnp.zeros((RIN, ROUT), F32)

    def gradients_of(head, slot):
        refs = (head, slot, qb, vb, gt, et, p_ref, l_ref, o_ref, accv, acck)
        gradient_block(0, True, *refs)

        @pl.loop(1, SEQ // GB)
        def _(block):
            gradient_block(pl.multiple_of(block * GB, GB), False, *refs)

        entry = et[...]
        value_part = dot(entry, accv[...].astype(BF16))
        key_part = dot(entry, acck[:, :HD].astype(BF16))
        query_part = dot(acck[:, HD:].astype(BF16), kb_ref[head], TN)
        query_part = query_part[:RIN] + query_part[RIN:]
        columns = pl.ds(pl.multiple_of(head * HD, HD), HD)
        sketch = None
        for kind, piece in enumerate((query_part, key_part, value_part)):
            term = dot_split(piece, fv[kind, columns, :])
            sketch = term if sketch is None else sketch + term
        part[1] += sketch * NORM

    @pl.loop(0, 2)
    def _(head):
        gradients_of(head, head)

    wait_head(2)
    softmax_of(2, 0)
    gradients_of(2, 0)

    @pl.loop(1, PEERS)
    def _(step):
        peer = peer_of(step)
        rows = pl.ds(pl.multiple_of(peer * 8, 8), 8)
        remote(part.at[:, rows, :], gather.at[s], r_send, r_recv, (f, peer)).start()

    gather[s] = part[:, pl.ds(pl.multiple_of(s * 8, 8), 8), :]
    seven = gather.at[pl.ds(0, PEERS - 1)]
    pltpu.make_async_copy(seven, seven, r_recv).wait()
    summed = jnp.sum(gather[...], axis=0)
    for sketch in range(2):
        for row in range(8):
            out[0, sketch : sketch + 1, row * 128 : (row + 1) * 128] = summed[
                sketch, row : row + 1, :
            ]

    pltpu.make_async_copy(seven, seven, r_send).wait()
    pltpu.make_async_copy(et.at[:, rest], et.at[:, rest], e_send).wait()
    for head in range(HPD):
        for which in range(3):
            sent = targets[which].at[head, rest]
            pltpu.make_async_copy(sent, sent, qkv_send.at[which, head]).wait()
    for copy in w_copies + [relay_up, relay_down]:
        copy.wait_send()
    for copy in (sg_mate, sg_across, sg_pass):
        copy.wait_send()
    for image in range(4):

        @pl.loop(0, RINGS)
        def _(chunk):
            far, _, peer = g_copies(chunk, image)
            if image == 0:

                @pl.when(peer != s)
                def _():
                    far.wait_send()
            else:
                far.wait_send()


def local(*operands):
    operands = list(operands)
    for place in (9, 11):
        operands[place] = operands[place].T
    dma = pltpu.SemaphoreType.DMA
    any_spec = pl.BlockSpec(memory_space=pl.ANY)
    in_specs = [any_spec] * 13
    in_specs[8] = pl.BlockSpec(memory_space=pltpu.SMEM)
    return pl.pallas_call(
        kernel,
        out_shape=jax.ShapeDtypeStruct((1, 2, RIN * ROUT // PEERS), F32),
        in_specs=in_specs,
        out_specs=pl.BlockSpec(memory_space=pltpu.VMEM),
        scratch_shapes=[
            pltpu.VMEM((HPD, SEQ, HD), BF16),
            pltpu.VMEM((HPD, SEQ, HD), BF16),
            pltpu.VMEM((HPD, SEQ, HD), BF16),
            pltpu.VMEM((HPD * HD, SEQ), BF16),
            pltpu.VMEM((RIN, SEQ), BF16),
            pltpu.VMEM((4, TOK, D), BF16),
            pltpu.VMEM((RINGS, WROWS, D), BF16),
            pltpu.VMEM((RINGS, 4, WROWS, TOK), BF16),
            pltpu.VMEM((TOK, D), BF16),
            pltpu.VMEM((TOK, D), BF16),
            pltpu.VMEM((64, D), F32),
            pltpu.VMEM((RIN, D), BF16),
            pltpu.VMEM((RIN, D), BF16),
            pltpu.VMEM((D, ROUT), BF16),
            pltpu.VMEM((3, HPD * HD, ROUT), BF16),
            pltpu.VMEM((2, SEQ, SB), F32),
            pltpu.VMEM((2, SEQ, SEQ), BF16),
            pltpu.VMEM((2, SEQ), F32),
            pltpu.VMEM((2, HD, SEQ), F32),
            pltpu.VMEM((HD, SEQ), BF16),
            pltpu.VMEM((SEQ, HD), F32),
            pltpu.VMEM((SEQ, 2 * HD), F32),
            pltpu.VMEM((2, RIN, ROUT), F32),
            pltpu.VMEM((PEERS, 2, 8, ROUT), F32),
            dma((11,)),
            dma((3, HPD)),
            dma((3, HPD)),
            dma((6,)),
            dma((6,)),
            dma((3,)),
            dma((3,)),
            dma,
            dma((16,)),
            dma,
            dma,
            dma,
            dma,
        ],
        compiler_params=pltpu.CompilerParams(
            collective_id=0, has_side_effects=True, vmem_limit_bytes=60 << 20
        ),
        cost_estimate=pl.CostEstimate(
            flops=26 * 10**9, bytes_accessed=16 * 2**20, transcendentals=13 * 10**6
        ),
    )(*operands)


def solution(mesh):
    in_specs = (
        P("fsdp", "seq", None),
        P("fsdp", "seq", None),
        P("fsdp", "seq", None),
        P("fsdp", "seq", None),
        P("fsdp", "seq", None),
        P("fsdp", "seq", None),
        P("fsdp", None),
        P(),
        P("fsdp"),
        P(),
        P(),
        P(),
        P(),
    )
    out_specs = P("fsdp", None, "seq")
    return jax.shard_map(local, mesh=mesh, in_specs=in_specs, out_specs=out_specs, check_vma=False)
```

```python
import math

import jax
import jax.numpy as jnp
from jax import lax
from jax.experimental import pallas as pl
from jax.experimental.pallas import tpu as pltpu
from jax.sharding import PartitionSpec as P

F32 = jnp.float32
BF16 = jnp.bfloat16
MESH = pl.DeviceIdType.MESH

D = 3072
HD = 128
TOK = 256
SEQ = 2048
PEERS = 8
HPD = 3
RIN = 64
ROUT = 128
WROWS = 192
HALF = 96
RINGS = 4
SCALE = 1.0 / math.sqrt(HD)
EXP2_SCALE = SCALE * math.log2(math.e)
NORM = 1.0 / math.sqrt(SEQ)
SB = 256
GB = 1024
KB = 256
KEY_STEPS = SEQ // KB

NN = (((1,), (0,)), ((), ()))
NT = (((1,), (1,)), ((), ()))
TN = (((0,), (0,)), ((), ()))


def dot(left, right, dims=NN, precision=None):
    return lax.dot_general(left, right, dims, precision=precision, preferred_element_type=F32)


def split(values):
    high = values.astype(BF16)
    return high, (values - high.astype(F32)).astype(BF16)


def dot_split(values, right, dims=NN):
    high, low = split(values)
    return dot(high, right, dims) + dot(low, right, dims)


def fold(values, reduce):
    rows, columns = values.shape
    return reduce(values.reshape(rows // 8, 8, columns), axis=0)


def values_of_head(head, slot, vb, et, p_ref, o_ref, vt):
    vt[:HD] = vb[head].T
    vt[HD:] = et[...]

    @pl.loop(0, SEQ // 512)
    def _(block):
        columns = pl.ds(pl.multiple_of(block * 512, 512), 512)
        o_ref[slot, :, columns] = dot(vt[...], p_ref[slot, :, columns])


def softmax_head(head, slot, with_values, qb, kb_ref, vb, et, s_ref, p_ref, l_ref, o_ref, vt):
    if with_values:
        vt[:HD] = vb[head].T
        vt[HD:] = et[...]

    def queries(start):
        wide = qb[head, pl.ds(start, SB), :].astype(F32).T
        return jnp.concatenate(split(wide * EXP2_SCALE), 0)

    def score(both, side, step, top):
        rows = pl.ds(step * KB, KB)
        keys = kb_ref[head, rows, :]
        scores = dot(jnp.concatenate([keys, keys], 1), both)
        s_ref[side, rows, :] = scores
        part = fold(scores, jnp.max)
        return part if top is None else jnp.maximum(top, part)

    def exponential(columns, side, step, top, total, mixed):
        rows = pl.ds(step * KB, KB)
        probs = jnp.exp2(s_ref[side, rows, :] - top)
        part = fold(probs, jnp.sum)
        probs = probs.astype(BF16)
        p_ref[slot, rows, columns] = probs
        total = part if total is None else total + part
        if with_values:
            piece = dot(vt[:, rows], probs)
            mixed = piece if mixed is None else mixed + piece
        return total, mixed

    def finish(columns, total, mixed):
        l_ref[pl.ds(slot, 1), columns] = jnp.sum(total, axis=0, keepdims=True)
        if with_values:
            o_ref[slot, :, columns] = mixed

    def highest(top):
        return jnp.max(top, axis=0, keepdims=True)

    def stage(block, side, top):
        columns = pl.ds(pl.multiple_of(block * SB, SB), SB)
        both = queries(pl.multiple_of((block + 1) * SB, SB))
        later, total, mixed = None, None, None
        for step in range(KEY_STEPS):
            later = score(both, 1 - side, step, later)
            total, mixed = exponential(columns, side, step, top, total, mixed)
        finish(columns, total, mixed)
        return highest(later)

    both, top = queries(0), None
    for step in range(KEY_STEPS):
        top = score(both, 0, step, top)
    blocks = SEQ // SB

    def pair(index, top):
        return stage(2 * index + 1, 1, stage(2 * index, 0, top))

    top = lax.fori_loop(0, blocks // 2 - 1, pair, highest(top))
    top = stage(blocks - 2, 0, top)
    columns = pl.ds(SEQ - SB, SB)
    total, mixed = None, None
    for step in range(KEY_STEPS):
        total, mixed = exponential(columns, 1, step, top, total, mixed)
    finish(columns, total, mixed)


def gradient_block(start, first, head, slot, qb, vb, gt, et, p_ref, l_ref, o_ref, accv, acck):
    columns = pl.ds(start, GB)
    inverse = 1.0 / l_ref[pl.ds(slot, 1), columns]
    grads = gt[pl.ds(pl.multiple_of(head * HD, HD), HD), columns]
    wide = grads.astype(F32)
    centre = jnp.sum(wide * o_ref[slot, :HD, columns], axis=0, keepdims=True) * inverse
    add_v = dot_split(o_ref[slot, HD:, columns] * inverse, grads, NT)
    if first:
        accv[...] = add_v
    else:
        accv[...] += add_v
    inverse = inverse * SCALE
    entry_high, entry_low = split(et[:, columns].astype(F32) * inverse)
    q_scaled = (qb[head, columns, :].astype(F32).T * inverse).astype(BF16)
    q_entry = jnp.concatenate([q_scaled, entry_high, entry_low], 0)
    for step in range(KEY_STEPS):
        rows = pl.ds(step * KB, KB)
        probs = p_ref[slot, rows, columns]
        prob_grad = dot(vb[head, rows, :], grads)
        score_grad = (probs.astype(F32) * (prob_grad - centre)).astype(BF16)
        add_k = dot(score_grad, q_entry, NT)
        if first:
            acck[rows, :] = add_k
        else:
            acck[rows, :] += add_k


def kernel(
    xn, qh, kh, vh, ao, og, wh, gates, step_ref, ef, mergedf, mixf, resf,
    out,
    qb, kb_ref, vb, gt, et, sg, wb, gst, xv, av, gv, efv, mfv, rfv, fv,
    s_ref, p_ref, l_ref, o_ref, vt, accv, acck, part, gather,
    load_sem, qkv_recv, qkv_send, w_recv, w_send, sg_recv, sg_send,
    g_recv, g_send, e_recv, e_send, r_recv, r_send,
):
    f = lax.axis_index("fsdp")
    s = lax.axis_index("seq")
    y = f // 4
    hi = (f // 2) % 2
    core = f % 2
    lo = s // 4
    zz = s % 4
    s_across = (1 - lo) * 4 + zz

    def heads_of(lo, z):
        return (2 * z + (lo + z) % 2) * HPD * HD

    mine = heads_of(lo, zz)
    mate = (f + 1 - 2 * core, s)
    across_f = y * 4 + (1 - hi) * 2 + core
    across = (across_f, s_across)
    up = ((f + 4) % 16, s)
    down = ((f + 12) % 16, s)

    barrier = pltpu.get_barrier_semaphore()

    for step in range(1, 32):
        target = (y * 4 + (f % 4 + step // 8) % 4, (s + step) % 8)
        pl.semaphore_signal(barrier, inc=1, device_id=target, device_id_type=MESH)

    for target in (up, down):
        pl.semaphore_signal(barrier, inc=1, device_id=target, device_id_type=MESH)

    loads = []

    def load(source, target):
        copy = pltpu.make_async_copy(source, target, load_sem.at[len(loads)])
        copy.start()
        loads.append(copy)
        return copy

    load_og = load(og.at[0], sg.at[0])
    load_gate = load(gates, gv)
    load_w = load(wh, wb.at[0])
    load_xn = load(xn.at[0], xv)
    load_ef = load(ef, efv)
    load_ao = load(ao.at[0], av)
    load_mf = load(mixf, mfv)
    load_rf = load(resf, rfv)
    load_f = [
        load(
            mergedf.at[pl.ds(pl.multiple_of(kind * D + mine, HD), HPD * HD), :], fv.at[kind]
        )
        for kind in range(3)
    ]

    sources = (qh, kh, vh)
    targets = (qb, kb_ref, vb)
    here = pl.ds(pl.multiple_of(s * TOK, TOK), TOK)
    for head in range(HPD):
        for which in range(3):
            columns = pl.ds(pl.multiple_of(mine + head * HD, HD), HD)
            pltpu.make_async_copy(
                sources[which].at[0, :, columns],
                targets[which].at[head, here, :],
                qkv_recv.at[which, head],
            ).start()

    pl.semaphore_wait(barrier, 33)

    def remote(source, target, send, recv, device):
        return pltpu.make_async_remote_copy(
            src_ref=source, dst_ref=target, send_sem=send, recv_sem=recv,
            device_id=device, device_id_type=MESH,
        )

    first_half = pl.ds(0, HALF)
    second_half = pl.ds(HALF, HALF)
    w_copies = [
        remote(wh.at[first_half], wb.at[2, first_half], w_send.at[0], w_recv.at[0], up),
        remote(wh.at[second_half], wb.at[1, second_half], w_send.at[1], w_recv.at[1], down),
        remote(wh.at[second_half], wb.at[2, second_half], w_send.at[2], w_recv.at[2], up),
        remote(wh.at[first_half], wb.at[1, first_half], w_send.at[3], w_recv.at[3], down),
    ]
    for copy in w_copies:
        copy.start()
    def peer_of(step):
        return ((lo + step // 4) % 2) * 4 + (zz + step) % 4

    def heads_of_peer(step):
        return heads_of((lo + step // 4) % 2, (zz + step) % 4)

    def send_head(head, kinds=(0, 1, 2)):
        @pl.loop(1, PEERS)
        def _(step):
            peer = peer_of(step)
            columns = pl.ds(pl.multiple_of(heads_of_peer(step) + head * HD, HD), HD)
            for which in kinds:
                remote(
                    sources[which].at[0, :, columns],
                    targets[which].at[head, here, :],
                    qkv_send.at[which, head],
                    qkv_recv.at[which, head],
                    (f, peer),
                ).start()

    send_head(0)

    load_og.wait()
    load_gate.wait()
    gate = gv[pl.ds(step_ref[0], 1), :]
    for row in range(0, TOK, 32):
        rows = pl.ds(row, 32)
        sg[0, rows, :] = (gate * sg[0, rows, :].astype(F32)).astype(BF16)

    sg_across = remote(sg.at[0], sg.at[2], sg_send.at[1], sg_recv.at[1], across)
    sg_across.start()
    sg_mate = remote(sg.at[0], sg.at[1], sg_send.at[0], sg_recv.at[0], mate)
    sg_mate.start()

    load_xn.wait()
    load_ef.wait()
    et[:, here] = dot(efv[...], xv[...], NT).astype(BF16)

    @pl.loop(1, PEERS)
    def _(step):
        peer = peer_of(step)
        remote(et.at[:, here], et.at[:, here], e_send, e_recv, (f, peer)).start()

    send_head(1)

    load_ao.wait()
    load_mf.wait()
    load_rf.wait()
    mixed_left = dot(mfv[...], av[...], NT)
    mixed_right = dot(sg[0], rfv[...])
    part[0] = dot(mixed_left, mixed_right, precision=lax.Precision.HIGHEST) * NORM

    def g_copies(place, image):
        chunk = (y + (0, 1, 3, 2)[place]) % 4
        token_block = s if image < 2 else s_across
        image_f = (f, mate[0], across_f, across_f + 1 - 2 * core)[image]
        peer = ((chunk + hi) % 2) * 4 + chunk
        columns = pl.ds(pl.multiple_of(token_block * TOK, TOK), TOK)
        target = gt.at[pl.ds(pl.multiple_of(core * WROWS, WROWS), WROWS), columns]
        source = gst.at[place, image]
        far = remote(source, target, g_send.at[place * 4 + image], g_recv, (image_f, peer))
        near = pltpu.make_async_copy(source, target, g_recv)
        return far, near, peer

    def make_g(first, last, image):
        weights = wb[first:last].reshape((last - first) * WROWS, D)
        grads = dot(weights, sg[image], NT).astype(BF16)
        for place in range(first, last):
            start = (place - first) * WROWS
            gst[place, image] = grads[start : start + WROWS]
            far, near, peer = g_copies(place, image)
            if image == 0:

                @pl.when(peer == s)
                def _():
                    near.start()

                @pl.when(peer != s)
                def _():
                    far.start()
            else:
                far.start()

    load_w.wait()
    make_g(0, 1, 0)
    sg_mate.wait_recv()
    make_g(0, 1, 1)
    w_copies[0].wait_recv()
    relay_up = remote(
        wb.at[2, first_half], wb.at[3, first_half], w_send.at[4], w_recv.at[4], up
    )
    relay_up.start()
    w_copies[1].wait_recv()
    relay_down = remote(
        wb.at[1, second_half], wb.at[3, second_half], w_send.at[5], w_recv.at[5], down
    )
    relay_down.start()

    def wait_head(head, kinds=(0, 1, 2)):
        for which in kinds:
            whole = targets[which].at[head]
            pltpu.make_async_copy(whole, whole, qkv_recv.at[which, head]).wait()

    def softmax_of(head, slot, with_values=True):
        softmax_head(
            head, slot, with_values, qb, kb_ref, vb, et, s_ref, p_ref, l_ref, o_ref, vt
        )

    rest = pl.ds(0, SEQ - TOK)
    pltpu.make_async_copy(et.at[:, rest], et.at[:, rest], e_recv).wait()
    wait_head(0)
    softmax_of(0, 0)
    w_copies[2].wait_recv()
    w_copies[3].wait_recv()


    make_g(1, 3, 0)
    make_g(1, 3, 1)
    sg_across.wait_recv()
    sg_pass = remote(sg.at[2], sg.at[3], sg_send.at[2], sg_recv.at[2], mate)
    sg_pass.start()
    make_g(0, 3, 2)
    relay_up.wait_recv()
    relay_down.wait_recv()
    for image in range(3):
        make_g(3, 4, image)
    sg_pass.wait_recv()
    make_g(0, 4, 3)
    send_head(2, (0, 1))
    send_head(2, (2,))
    wait_head(1)
    softmax_of(1, 1)

    for copy in load_f:
        copy.wait()
    pltpu.make_async_copy(gt, gt, g_recv).wait()
    part[1] = jnp.zeros((RIN, ROUT), F32)

    def gradients_of(head, slot):
        refs = (head, slot, qb, vb, gt, et, p_ref, l_ref, o_ref, accv, acck)
        gradient_block(0, True, *refs)

        @pl.loop(1, SEQ // GB)
        def _(block):
            gradient_block(pl.multiple_of(block * GB, GB), False, *refs)

        entry = et[...]
        value_part = accv[...]
        key_part = dot(entry, acck[:, :HD].astype(BF16))
        query_part = dot(acck[:, HD:].astype(BF16), kb_ref[head], TN)
        query_part = query_part[:RIN] + query_part[RIN:]
        columns = pl.ds(pl.multiple_of(head * HD, HD), HD)
        sketch = None
        for kind, piece in enumerate((query_part, key_part, value_part)):
            term = dot_split(piece, fv[kind, columns, :])
            sketch = term if sketch is None else sketch + term
        part[1] += sketch * NORM

    @pl.loop(0, 2)
    def _(head):
        gradients_of(head, head)

    wait_head(2, (0, 1))
    softmax_of(2, 0, False)
    wait_head(2, (2,))
    values_of_head(2, 0, vb, et, p_ref, o_ref, vt)
    gradients_of(2, 0)

    @pl.loop(1, PEERS)
    def _(step):
        peer = peer_of(step)
        rows = pl.ds(pl.multiple_of(peer * 8, 8), 8)
        remote(part.at[:, rows, :], gather.at[s], r_send, r_recv, (f, peer)).start()

    gather[s] = part[:, pl.ds(pl.multiple_of(s * 8, 8), 8), :]
    seven = gather.at[pl.ds(0, PEERS - 1)]
    pltpu.make_async_copy(seven, seven, r_recv).wait()
    summed = jnp.sum(gather[...], axis=0)
    for sketch in range(2):
        for row in range(8):
            out[0, sketch : sketch + 1, row * 128 : (row + 1) * 128] = summed[
                sketch, row : row + 1, :
            ]

    pltpu.make_async_copy(seven, seven, r_send).wait()
    pltpu.make_async_copy(et.at[:, rest], et.at[:, rest], e_send).wait()
    for head in range(HPD):
        for which in range(3):
            sent = targets[which].at[head, rest]
            pltpu.make_async_copy(sent, sent, qkv_send.at[which, head]).wait()
    for copy in w_copies + [relay_up, relay_down]:
        copy.wait_send()
    for copy in (sg_mate, sg_across, sg_pass):
        copy.wait_send()
    for image in range(4):
        for place in range(RINGS):
            far, _, peer = g_copies(place, image)
            if image == 0:
                pl.when(peer != s)(far.wait_send)
            else:
                far.wait_send()


def local(*operands):
    operands = list(operands)
    for place in (9, 11):
        operands[place] = operands[place].T
    dma = pltpu.SemaphoreType.DMA
    any_spec = pl.BlockSpec(memory_space=pl.ANY)
    in_specs = [any_spec] * 13
    in_specs[8] = pl.BlockSpec(memory_space=pltpu.SMEM)
    return pl.pallas_call(
        kernel,
        out_shape=jax.ShapeDtypeStruct((1, 2, RIN * ROUT // PEERS), F32),
        in_specs=in_specs,
        out_specs=pl.BlockSpec(memory_space=pltpu.VMEM),
        scratch_shapes=[
            pltpu.VMEM((HPD, SEQ, HD), BF16),
            pltpu.VMEM((HPD, SEQ, HD), BF16),
            pltpu.VMEM((HPD, SEQ, HD), BF16),
            pltpu.VMEM((HPD * HD, SEQ), BF16),
            pltpu.VMEM((RIN, SEQ), BF16),
            pltpu.VMEM((4, TOK, D), BF16),
            pltpu.VMEM((RINGS, WROWS, D), BF16),
            pltpu.VMEM((RINGS, 4, WROWS, TOK), BF16),
            pltpu.VMEM((TOK, D), BF16),
            pltpu.VMEM((TOK, D), BF16),
            pltpu.VMEM((64, D), F32),
            pltpu.VMEM((RIN, D), BF16),
            pltpu.VMEM((RIN, D), BF16),
            pltpu.VMEM((D, ROUT), BF16),
            pltpu.VMEM((3, HPD * HD, ROUT), BF16),
            pltpu.VMEM((2, SEQ, SB), F32),
            pltpu.VMEM((2, SEQ, SEQ), BF16),
            pltpu.VMEM((2, SEQ), F32),
            pltpu.VMEM((2, HD + RIN, SEQ), F32),
            pltpu.VMEM((HD + RIN, SEQ), BF16),
            pltpu.VMEM((RIN, HD), F32),
            pltpu.VMEM((SEQ, 2 * HD), F32),
            pltpu.VMEM((2, RIN, ROUT), F32),
            pltpu.VMEM((PEERS, 2, 8, ROUT), F32),
            dma((11,)),
            dma((3, HPD)),
            dma((3, HPD)),
            dma((6,)),
            dma((6,)),
            dma((3,)),
            dma((3,)),
            dma,
            dma((16,)),
            dma,
            dma,
            dma,
            dma,
        ],
        compiler_params=pltpu.CompilerParams(
            collective_id=0, has_side_effects=True, vmem_limit_bytes=60 << 20
        ),
        cost_estimate=pl.CostEstimate(
            flops=26 * 10**9, bytes_accessed=16 * 2**20, transcendentals=13 * 10**6
        ),
    )(*operands)


def solution(mesh):
    in_specs = (
        P("fsdp", "seq", None),
        P("fsdp", "seq", None),
        P("fsdp", "seq", None),
        P("fsdp", "seq", None),
        P("fsdp", "seq", None),
        P("fsdp", "seq", None),
        P("fsdp", None),
        P(),
        P("fsdp"),
        P(),
        P(),
        P(),
        P(),
    )
    out_specs = P("fsdp", None, "seq")
    return jax.shard_map(local, mesh=mesh, in_specs=in_specs, out_specs=out_specs, check_vma=False)
```

```python
import math

import jax
import jax.numpy as jnp
from jax import lax
from jax.experimental import pallas as pl
from jax.experimental.pallas import tpu as pltpu
from jax.sharding import PartitionSpec as P

F32 = jnp.float32
BF16 = jnp.bfloat16
MESH = pl.DeviceIdType.MESH

D = 3072
HD = 128
TOK = 256
SEQ = 2048
PEERS = 8
HPD = 3
RIN = 64
ROUT = 128
WROWS = 192
HALF = 96
RINGS = 4
SCALE = 1.0 / math.sqrt(HD)
EXP2_SCALE = SCALE * math.log2(math.e)
NORM = 1.0 / math.sqrt(SEQ)
SB = 256
GB = 1024
KB = 256
KEY_STEPS = SEQ // KB

NN = (((1,), (0,)), ((), ()))
NT = (((1,), (1,)), ((), ()))
TN = (((0,), (0,)), ((), ()))


def dot(left, right, dims=NN, precision=None):
    return lax.dot_general(left, right, dims, precision=precision, preferred_element_type=F32)


def split(values):
    high = values.astype(BF16)
    return high, (values - high.astype(F32)).astype(BF16)


def dot_split(values, right, dims=NN):
    high, low = split(values)
    return dot(high, right, dims) + dot(low, right, dims)


def fold(values, reduce):
    rows, columns = values.shape
    return reduce(values.reshape(rows // 8, 8, columns), axis=0)


def values_of_half(head, slot, base, first, vb, et, p_ref, o_ref, vt):
    half = SEQ // 2
    rows = pl.ds(base, half)
    vt[:HD, :half] = vb[head, rows, :].T
    vt[HD:, :half] = et[:, rows]

    @pl.loop(0, SEQ // 512)
    def _(block):
        columns = pl.ds(pl.multiple_of(block * 512, 512), 512)
        mixed = dot(vt[:, :half], p_ref[slot, rows, columns])
        if first:
            o_ref[slot, :, columns] = mixed
        else:
            o_ref[slot, :, columns] += mixed


def softmax_head(head, slot, with_values, qb, kb_ref, vb, et, s_ref, p_ref, l_ref, o_ref, vt):
    if with_values:
        vt[:HD] = vb[head].T
        vt[HD:] = et[...]

    def queries(start):
        wide = qb[head, pl.ds(start, SB), :].astype(F32).T
        return jnp.concatenate(split(wide * EXP2_SCALE), 0)

    def score(both, side, step, top):
        rows = pl.ds(step * KB, KB)
        keys = kb_ref[head, rows, :]
        scores = dot(jnp.concatenate([keys, keys], 1), both)
        s_ref[side, rows, :] = scores
        part = fold(scores, jnp.max)
        return part if top is None else jnp.maximum(top, part)

    def exponential(columns, side, step, top, total, mixed):
        rows = pl.ds(step * KB, KB)
        probs = jnp.exp2(s_ref[side, rows, :] - top)
        part = fold(probs, jnp.sum)
        probs = probs.astype(BF16)
        p_ref[slot, rows, columns] = probs
        total = part if total is None else total + part
        if with_values:
            piece = dot(vt[:, rows], probs)
            mixed = piece if mixed is None else mixed + piece
        return total, mixed

    def finish(columns, total, mixed):
        l_ref[pl.ds(slot, 1), columns] = jnp.sum(total, axis=0, keepdims=True)
        if with_values:
            o_ref[slot, :, columns] = mixed

    def highest(top):
        return jnp.max(top, axis=0, keepdims=True)

    def stage(block, side, top):
        columns = pl.ds(pl.multiple_of(block * SB, SB), SB)
        both = queries(pl.multiple_of((block + 1) * SB, SB))
        later, total, mixed = None, None, None
        for step in range(KEY_STEPS):
            later = score(both, 1 - side, step, later)
            total, mixed = exponential(columns, side, step, top, total, mixed)
        finish(columns, total, mixed)
        return highest(later)

    both, top = queries(0), None
    for step in range(KEY_STEPS):
        top = score(both, 0, step, top)
    blocks = SEQ // SB

    def pair(index, top):
        return stage(2 * index + 1, 1, stage(2 * index, 0, top))

    top = lax.fori_loop(0, blocks // 2 - 1, pair, highest(top))
    top = stage(blocks - 2, 0, top)
    columns = pl.ds(SEQ - SB, SB)
    total, mixed = None, None
    for step in range(KEY_STEPS):
        total, mixed = exponential(columns, 1, step, top, total, mixed)
    finish(columns, total, mixed)


def gradient_block(start, first, head, slot, qb, vb, gt, et, p_ref, l_ref, o_ref, accv, acck):
    columns = pl.ds(start, GB)
    inverse = 1.0 / l_ref[pl.ds(slot, 1), columns]
    grads = gt[pl.ds(pl.multiple_of(head * HD, HD), HD), columns]
    wide = grads.astype(F32)
    centre = jnp.sum(wide * o_ref[slot, :HD, columns], axis=0, keepdims=True) * inverse
    add_v = dot_split(o_ref[slot, HD:, columns] * inverse, grads, NT)
    if first:
        accv[...] = add_v
    else:
        accv[...] += add_v
    inverse = inverse * SCALE
    entry_high, entry_low = split(et[:, columns].astype(F32) * inverse)
    q_scaled = (qb[head, columns, :].astype(F32).T * inverse).astype(BF16)
    q_entry = jnp.concatenate([q_scaled, entry_high, entry_low], 0)
    for step in range(KEY_STEPS):
        rows = pl.ds(step * KB, KB)
        probs = p_ref[slot, rows, columns]
        prob_grad = dot(vb[head, rows, :], grads)
        score_grad = (probs.astype(F32) * (prob_grad - centre)).astype(BF16)
        add_k = dot(score_grad, q_entry, NT)
        if first:
            acck[rows, :] = add_k
        else:
            acck[rows, :] += add_k


def kernel(
    xn, qh, kh, vh, ao, og, wh, gates, step_ref, ef, mergedf, mixf, resf,
    out,
    qb, kb_ref, vb, gt, et, sg, wb, gst, xv, av, gv, efv, mfv, rfv, fv,
    s_ref, p_ref, l_ref, o_ref, vt, accv, acck, part, gather,
    load_sem, qkv_recv, late_recv, qkv_send, w_recv, w_send, sg_recv, sg_send,
    g_recv, g_send, e_recv, e_send, r_recv, r_send,
):
    f = lax.axis_index("fsdp")
    s = lax.axis_index("seq")
    y = f // 4
    hi = (f // 2) % 2
    core = f % 2
    lo = s // 4
    zz = s % 4
    s_across = (1 - lo) * 4 + zz

    def heads_of(lo, z):
        return (2 * z + (lo + z) % 2) * HPD * HD

    mine = heads_of(lo, zz)
    mate = (f + 1 - 2 * core, s)
    across_f = y * 4 + (1 - hi) * 2 + core
    across = (across_f, s_across)
    up = ((f + 4) % 16, s)
    down = ((f + 12) % 16, s)

    barrier = pltpu.get_barrier_semaphore()

    for step in range(1, 32):
        target = (y * 4 + (f % 4 + step // 8) % 4, (s + step) % 8)
        pl.semaphore_signal(barrier, inc=1, device_id=target, device_id_type=MESH)

    for target in (up, down):
        pl.semaphore_signal(barrier, inc=1, device_id=target, device_id_type=MESH)

    loads = []

    def load(source, target):
        copy = pltpu.make_async_copy(source, target, load_sem.at[len(loads)])
        copy.start()
        loads.append(copy)
        return copy

    load_og = load(og.at[0], sg.at[0])
    load_gate = load(gates, gv)
    load_w = load(wh, wb.at[0])
    load_xn = load(xn.at[0], xv)
    load_ef = load(ef, efv)
    load_ao = load(ao.at[0], av)
    load_mf = load(mixf, mfv)
    load_rf = load(resf, rfv)
    load_f = [
        load(
            mergedf.at[pl.ds(pl.multiple_of(kind * D + mine, HD), HPD * HD), :], fv.at[kind]
        )
        for kind in range(3)
    ]

    sources = (qh, kh, vh)
    targets = (qb, kb_ref, vb)
    here = pl.ds(pl.multiple_of(s * TOK, TOK), TOK)
    for head in range(HPD):
        for which in range(3):
            columns = pl.ds(pl.multiple_of(mine + head * HD, HD), HD)
            pltpu.make_async_copy(
                sources[which].at[0, :, columns],
                targets[which].at[head, here, :],
                qkv_recv.at[which, head],
            ).start()

    pl.semaphore_wait(barrier, 33)

    def remote(source, target, send, recv, device):
        return pltpu.make_async_remote_copy(
            src_ref=source, dst_ref=target, send_sem=send, recv_sem=recv,
            device_id=device, device_id_type=MESH,
        )

    first_half = pl.ds(0, HALF)
    second_half = pl.ds(HALF, HALF)
    w_copies = [
        remote(wh.at[first_half], wb.at[2, first_half], w_send.at[0], w_recv.at[0], up),
        remote(wh.at[second_half], wb.at[1, second_half], w_send.at[1], w_recv.at[1], down),
        remote(wh.at[second_half], wb.at[2, second_half], w_send.at[2], w_recv.at[2], up),
        remote(wh.at[first_half], wb.at[1, first_half], w_send.at[3], w_recv.at[3], down),
    ]
    for copy in w_copies:
        copy.start()
    def peer_of(step):
        return ((lo + step // 4) % 2) * 4 + (zz + step) % 4

    def heads_of_peer(step):
        return heads_of((lo + step // 4) % 2, (zz + step) % 4)

    def send_head(head, kinds=(0, 1, 2), first=1, last=PEERS, late=False):
        @pl.loop(first, last)
        def _(step):
            peer = peer_of(step)
            columns = pl.ds(pl.multiple_of(heads_of_peer(step) + head * HD, HD), HD)
            for which in kinds:
                remote(
                    sources[which].at[0, :, columns],
                    targets[which].at[head, here, :],
                    qkv_send.at[which, head],
                    late_recv if late else qkv_recv.at[which, head],
                    (f, peer),
                ).start()

    send_head(0)

    load_og.wait()
    load_gate.wait()
    gate = gv[pl.ds(step_ref[0], 1), :]
    for row in range(0, TOK, 32):
        rows = pl.ds(row, 32)
        sg[0, rows, :] = (gate * sg[0, rows, :].astype(F32)).astype(BF16)

    sg_across = remote(sg.at[0], sg.at[2], sg_send.at[1], sg_recv.at[1], across)
    sg_across.start()
    sg_mate = remote(sg.at[0], sg.at[1], sg_send.at[0], sg_recv.at[0], mate)
    sg_mate.start()

    load_xn.wait()
    load_ef.wait()
    et[:, here] = dot(efv[...], xv[...], NT).astype(BF16)

    @pl.loop(1, PEERS)
    def _(step):
        peer = peer_of(step)
        remote(et.at[:, here], et.at[:, here], e_send, e_recv, (f, peer)).start()

    send_head(1)

    load_ao.wait()
    load_mf.wait()
    load_rf.wait()
    mixed_left = dot(mfv[...], av[...], NT)
    mixed_right = dot(sg[0], rfv[...])
    part[0] = dot(mixed_left, mixed_right, precision=lax.Precision.HIGHEST) * NORM

    def g_copies(place, image):
        chunk = (y + (0, 1, 3, 2)[place]) % 4
        token_block = s if image < 2 else s_across
        image_f = (f, mate[0], across_f, across_f + 1 - 2 * core)[image]
        peer = ((chunk + hi) % 2) * 4 + chunk
        columns = pl.ds(pl.multiple_of(token_block * TOK, TOK), TOK)
        target = gt.at[pl.ds(pl.multiple_of(core * WROWS, WROWS), WROWS), columns]
        source = gst.at[place, image]
        far = remote(source, target, g_send.at[place * 4 + image], g_recv, (image_f, peer))
        near = pltpu.make_async_copy(source, target, g_recv)
        return far, near, peer

    def make_g(first, last, image):
        weights = wb[first:last].reshape((last - first) * WROWS, D)
        grads = dot(weights, sg[image], NT).astype(BF16)
        for place in range(first, last):
            start = (place - first) * WROWS
            gst[place, image] = grads[start : start + WROWS]
            far, near, peer = g_copies(place, image)
            if image == 0:

                @pl.when(peer == s)
                def _():
                    near.start()

                @pl.when(peer != s)
                def _():
                    far.start()
            else:
                far.start()

    load_w.wait()
    make_g(0, 1, 0)
    sg_mate.wait_recv()
    make_g(0, 1, 1)
    w_copies[0].wait_recv()
    relay_up = remote(
        wb.at[2, first_half], wb.at[3, first_half], w_send.at[4], w_recv.at[4], up
    )
    relay_up.start()
    w_copies[1].wait_recv()
    relay_down = remote(
        wb.at[1, second_half], wb.at[3, second_half], w_send.at[5], w_recv.at[5], down
    )
    relay_down.start()

    def wait_head(head, kinds=(0, 1, 2)):
        for which in kinds:
            whole = targets[which].at[head]
            pltpu.make_async_copy(whole, whole, qkv_recv.at[which, head]).wait()

    def softmax_of(head, slot, with_values=True):
        softmax_head(
            head, slot, with_values, qb, kb_ref, vb, et, s_ref, p_ref, l_ref, o_ref, vt
        )

    rest = pl.ds(0, SEQ - TOK)
    pltpu.make_async_copy(et.at[:, rest], et.at[:, rest], e_recv).wait()
    wait_head(0)
    softmax_of(0, 0)
    w_copies[2].wait_recv()
    w_copies[3].wait_recv()


    make_g(1, 3, 0)
    make_g(1, 3, 1)
    sg_across.wait_recv()
    sg_pass = remote(sg.at[2], sg.at[3], sg_send.at[2], sg_recv.at[2], mate)
    sg_pass.start()
    make_g(0, 3, 2)
    relay_up.wait_recv()
    relay_down.wait_recv()
    for image in range(3):
        make_g(3, 4, image)
    sg_pass.wait_recv()
    make_g(0, 4, 3)
    send_head(2, (0, 1))
    send_head(2, (2,), 1, 4)
    send_head(2, (2,), 4, PEERS, True)
    wait_head(1)
    softmax_of(1, 1)

    for copy in load_f:
        copy.wait()
    pltpu.make_async_copy(gt, gt, g_recv).wait()
    part[1] = jnp.zeros((RIN, ROUT), F32)

    def gradients_of(head, slot):
        refs = (head, slot, qb, vb, gt, et, p_ref, l_ref, o_ref, accv, acck)
        gradient_block(0, True, *refs)

        @pl.loop(1, SEQ // GB)
        def _(block):
            gradient_block(pl.multiple_of(block * GB, GB), False, *refs)

        entry = et[...]
        value_part = accv[...]
        key_part = dot(entry, acck[:, :HD].astype(BF16))
        query_part = dot(acck[:, HD:].astype(BF16), kb_ref[head], TN)
        query_part = query_part[:RIN] + query_part[RIN:]
        columns = pl.ds(pl.multiple_of(head * HD, HD), HD)
        sketch = None
        for kind, piece in enumerate((query_part, key_part, value_part)):
            term = dot_split(piece, fv[kind, columns, :])
            sketch = term if sketch is None else sketch + term
        part[1] += sketch * NORM

    @pl.loop(0, 2)
    def _(head):
        gradients_of(head, head)

    wait_head(2, (0, 1))
    softmax_of(2, 0, False)
    halves = [pl.multiple_of(((lo + turn) % 2) * (SEQ // 2), SEQ // 2) for turn in range(2)]
    for turn, arrived in enumerate((qkv_recv.at[2, 2], late_recv)):
        part_values = vb.at[2, pl.ds(halves[turn], SEQ // 2)]
        pltpu.make_async_copy(part_values, part_values, arrived).wait()
        values_of_half(2, 0, halves[turn], turn == 0, vb, et, p_ref, o_ref, vt)
    gradients_of(2, 0)

    @pl.loop(1, PEERS)
    def _(step):
        peer = peer_of(step)
        rows = pl.ds(pl.multiple_of(peer * 8, 8), 8)
        remote(part.at[:, rows, :], gather.at[s], r_send, r_recv, (f, peer)).start()

    gather[s] = part[:, pl.ds(pl.multiple_of(s * 8, 8), 8), :]
    seven = gather.at[pl.ds(0, PEERS - 1)]
    pltpu.make_async_copy(seven, seven, r_recv).wait()
    summed = jnp.sum(gather[...], axis=0)
    for sketch in range(2):
        for row in range(8):
            out[0, sketch : sketch + 1, row * 128 : (row + 1) * 128] = summed[
                sketch, row : row + 1, :
            ]

    pltpu.make_async_copy(seven, seven, r_send).wait()
    pltpu.make_async_copy(et.at[:, rest], et.at[:, rest], e_send).wait()
    for head in range(HPD):
        for which in range(3):
            sent = targets[which].at[head, rest]
            pltpu.make_async_copy(sent, sent, qkv_send.at[which, head]).wait()
    for copy in w_copies + [relay_up, relay_down]:
        copy.wait_send()
    for copy in (sg_mate, sg_across, sg_pass):
        copy.wait_send()
    for image in range(4):
        for place in range(RINGS):
            far, _, peer = g_copies(place, image)
            if image == 0:
                pl.when(peer != s)(far.wait_send)
            else:
                far.wait_send()


def local(*operands):
    operands = list(operands)
    for place in (9, 11):
        operands[place] = operands[place].T
    dma = pltpu.SemaphoreType.DMA
    any_spec = pl.BlockSpec(memory_space=pl.ANY)
    in_specs = [any_spec] * 13
    in_specs[8] = pl.BlockSpec(memory_space=pltpu.SMEM)
    return pl.pallas_call(
        kernel,
        out_shape=jax.ShapeDtypeStruct((1, 2, RIN * ROUT // PEERS), F32),
        in_specs=in_specs,
        out_specs=pl.BlockSpec(memory_space=pltpu.VMEM),
        scratch_shapes=[
            pltpu.VMEM((HPD, SEQ, HD), BF16),
            pltpu.VMEM((HPD, SEQ, HD), BF16),
            pltpu.VMEM((HPD, SEQ, HD), BF16),
            pltpu.VMEM((HPD * HD, SEQ), BF16),
            pltpu.VMEM((RIN, SEQ), BF16),
            pltpu.VMEM((4, TOK, D), BF16),
            pltpu.VMEM((RINGS, WROWS, D), BF16),
            pltpu.VMEM((RINGS, 4, WROWS, TOK), BF16),
            pltpu.VMEM((TOK, D), BF16),
            pltpu.VMEM((TOK, D), BF16),
            pltpu.VMEM((64, D), F32),
            pltpu.VMEM((RIN, D), BF16),
            pltpu.VMEM((RIN, D), BF16),
            pltpu.VMEM((D, ROUT), BF16),
            pltpu.VMEM((3, HPD * HD, ROUT), BF16),
            pltpu.VMEM((2, SEQ, SB), F32),
            pltpu.VMEM((2, SEQ, SEQ), BF16),
            pltpu.VMEM((2, SEQ), F32),
            pltpu.VMEM((2, HD + RIN, SEQ), F32),
            pltpu.VMEM((HD + RIN, SEQ), BF16),
            pltpu.VMEM((RIN, HD), F32),
            pltpu.VMEM((SEQ, 2 * HD), F32),
            pltpu.VMEM((2, RIN, ROUT), F32),
            pltpu.VMEM((PEERS, 2, 8, ROUT), F32),
            dma((11,)),
            dma((3, HPD)),
            dma,
            dma((3, HPD)),
            dma((6,)),
            dma((6,)),
            dma((3,)),
            dma((3,)),
            dma,
            dma((16,)),
            dma,
            dma,
            dma,
            dma,
        ],
        compiler_params=pltpu.CompilerParams(
            collective_id=0, has_side_effects=True, vmem_limit_bytes=60 << 20
        ),
        cost_estimate=pl.CostEstimate(
            flops=26 * 10**9, bytes_accessed=16 * 2**20, transcendentals=13 * 10**6
        ),
    )(*operands)


def solution(mesh):
    in_specs = (
        P("fsdp", "seq", None),
        P("fsdp", "seq", None),
        P("fsdp", "seq", None),
        P("fsdp", "seq", None),
        P("fsdp", "seq", None),
        P("fsdp", "seq", None),
        P("fsdp", None),
        P(),
        P("fsdp"),
        P(),
        P(),
        P(),
        P(),
    )
    out_specs = P("fsdp", None, "seq")
    return jax.shard_map(local, mesh=mesh, in_specs=in_specs, out_specs=out_specs, check_vma=False)
```

```python
import math

import jax
import jax.numpy as jnp
from jax import lax
from jax.experimental import pallas as pl
from jax.experimental.pallas import tpu as pltpu
from jax.sharding import PartitionSpec as P

F32 = jnp.float32
BF16 = jnp.bfloat16
MESH = pl.DeviceIdType.MESH

D = 3072
HD = 128
TOK = 256
SEQ = 2048
PEERS = 8
HPD = 3
RIN = 64
ROUT = 128
WROWS = 192
HALF = 96
RINGS = 4
SCALE = 1.0 / math.sqrt(HD)
EXP2_SCALE = SCALE * math.log2(math.e)
NORM = 1.0 / math.sqrt(SEQ)
SB = 256
GB = 1024
KB = 256
KEY_STEPS = SEQ // KB

NN = (((1,), (0,)), ((), ()))
NT = (((1,), (1,)), ((), ()))
TN = (((0,), (0,)), ((), ()))


def dot(left, right, dims=NN, precision=None):
    return lax.dot_general(left, right, dims, precision=precision, preferred_element_type=F32)


def split(values):
    high = values.astype(BF16)
    return high, (values - high.astype(F32)).astype(BF16)


def dot_split(values, right, dims=NN):
    high, low = split(values)
    return dot(high, right, dims) + dot(low, right, dims)


def fold(values, reduce):
    rows, columns = values.shape
    return reduce(values.reshape(rows // 8, 8, columns), axis=0)


def values_of_head(head, slot, vb, et, p_ref, o_ref, vt):
    vt[:HD] = vb[head].T
    vt[HD:] = et[...]

    @pl.loop(0, SEQ // 512)
    def _(block):
        columns = pl.ds(pl.multiple_of(block * 512, 512), 512)
        o_ref[slot, :, columns] = dot(vt[...], p_ref[slot, :, columns])


def softmax_head(head, slot, with_values, qb, kb_ref, vb, et, s_ref, p_ref, l_ref, o_ref, vt):
    if with_values:
        vt[:HD] = vb[head].T
        vt[HD:] = et[...]

    def queries(start):
        wide = qb[head, pl.ds(start, SB), :].astype(F32).T
        return jnp.concatenate(split(wide * EXP2_SCALE), 0)

    def score(both, side, step, top):
        rows = pl.ds(step * KB, KB)
        keys = kb_ref[head, rows, :]
        scores = dot(jnp.concatenate([keys, keys], 1), both)
        s_ref[side, rows, :] = scores
        part = fold(scores, jnp.max)
        return part if top is None else jnp.maximum(top, part)

    def exponential(columns, side, step, top, total, mixed):
        rows = pl.ds(step * KB, KB)
        probs = jnp.exp2(s_ref[side, rows, :] - top)
        part = fold(probs, jnp.sum)
        probs = probs.astype(BF16)
        p_ref[slot, rows, columns] = probs
        total = part if total is None else total + part
        if with_values:
            piece = dot(vt[:, rows], probs)
            mixed = piece if mixed is None else mixed + piece
        return total, mixed

    def finish(columns, total, mixed):
        l_ref[pl.ds(slot, 1), columns] = jnp.sum(total, axis=0, keepdims=True)
        if with_values:
            o_ref[slot, :, columns] = mixed

    def highest(top):
        return jnp.max(top, axis=0, keepdims=True)

    def stage(block, side, top):
        columns = pl.ds(pl.multiple_of(block * SB, SB), SB)
        both = queries(pl.multiple_of((block + 1) * SB, SB))
        later, total, mixed = None, None, None
        for step in range(KEY_STEPS):
            later = score(both, 1 - side, step, later)
            total, mixed = exponential(columns, side, step, top, total, mixed)
        finish(columns, total, mixed)
        return highest(later)

    both, top = queries(0), None
    for step in range(KEY_STEPS):
        top = score(both, 0, step, top)
    blocks = SEQ // SB

    def pair(index, top):
        return stage(2 * index + 1, 1, stage(2 * index, 0, top))

    top = lax.fori_loop(0, blocks // 2 - 1, pair, highest(top))
    top = stage(blocks - 2, 0, top)
    columns = pl.ds(SEQ - SB, SB)
    total, mixed = None, None
    for step in range(KEY_STEPS):
        total, mixed = exponential(columns, 1, step, top, total, mixed)
    finish(columns, total, mixed)


def gradient_block(start, first, head, slot, qb, vb, gt, et, p_ref, l_ref, o_ref, accv, acck):
    columns = pl.ds(start, GB)
    inverse = 1.0 / l_ref[pl.ds(slot, 1), columns]
    grads = gt[pl.ds(pl.multiple_of(head * HD, HD), HD), columns]
    wide = grads.astype(F32)
    centre = jnp.sum(wide * o_ref[slot, :HD, columns], axis=0, keepdims=True) * inverse
    add_v = dot_split(o_ref[slot, HD:, columns] * inverse, grads, NT)
    if first:
        accv[...] = add_v
    else:
        accv[...] += add_v
    inverse = inverse * SCALE
    entry_high, entry_low = split(et[:, columns].astype(F32) * inverse)
    q_scaled = (qb[head, columns, :].astype(F32).T * inverse).astype(BF16)
    q_entry = jnp.concatenate([q_scaled, entry_high, entry_low], 0)
    for step in range(KEY_STEPS):
        rows = pl.ds(step * KB, KB)
        probs = p_ref[slot, rows, columns]
        prob_grad = dot(vb[head, rows, :], grads)
        score_grad = (probs.astype(F32) * (prob_grad - centre)).astype(BF16)
        add_k = dot(score_grad, q_entry, NT)
        if first:
            acck[rows, :] = add_k
        else:
            acck[rows, :] += add_k


def kernel(
    xn, qh, kh, vh, ao, og, wh, gates, step_ref, ef, mergedf, mixf, resf,
    out,
    qb, kb_ref, vb, gt, et, sg, wb, gst, xv, av, gv, efv, mfv, rfv, fv,
    s_ref, p_ref, l_ref, o_ref, vt, accv, acck, part, gather,
    load_sem, qkv_recv, qkv_send, w_recv, w_send, sg_recv, sg_send,
    g_recv, g_send, e_recv, e_send, r_recv, r_send,
):
    f = lax.axis_index("fsdp")
    s = lax.axis_index("seq")
    y = f // 4
    hi = (f // 2) % 2
    core = f % 2
    lo = s // 4
    zz = s % 4
    s_across = (1 - lo) * 4 + zz

    def heads_of(lo, z):
        return (2 * z + (lo + z) % 2) * HPD * HD

    mine = heads_of(lo, zz)
    mate = (f + 1 - 2 * core, s)
    across_f = y * 4 + (1 - hi) * 2 + core
    across = (across_f, s_across)
    up = ((f + 4) % 16, s)
    down = ((f + 12) % 16, s)

    barrier = pltpu.get_barrier_semaphore()

    for step in range(1, 32):
        target = (y * 4 + (f % 4 + step // 8) % 4, (s + step) % 8)
        pl.semaphore_signal(barrier, inc=1, device_id=target, device_id_type=MESH)

    for target in (up, down):
        pl.semaphore_signal(barrier, inc=1, device_id=target, device_id_type=MESH)

    loads = []

    def load(source, target):
        copy = pltpu.make_async_copy(source, target, load_sem.at[len(loads)])
        copy.start()
        loads.append(copy)
        return copy

    load_og = load(og.at[0], sg.at[0])
    load_gate = load(gates, gv)
    load_w = load(wh, wb.at[0])

    sources = (qh, kh, vh)
    targets = (qb, kb_ref, vb)
    here = pl.ds(pl.multiple_of(s * TOK, TOK), TOK)
    pl.semaphore_wait(barrier, 33)

    def remote(source, target, send, recv, device):
        return pltpu.make_async_remote_copy(
            src_ref=source, dst_ref=target, send_sem=send, recv_sem=recv,
            device_id=device, device_id_type=MESH,
        )

    first_half = pl.ds(0, HALF)
    second_half = pl.ds(HALF, HALF)
    w_copies = [
        remote(wh.at[first_half], wb.at[2, first_half], w_send.at[0], w_recv.at[0], up),
        remote(wh.at[second_half], wb.at[1, second_half], w_send.at[1], w_recv.at[1], down),
        remote(wh.at[second_half], wb.at[2, second_half], w_send.at[2], w_recv.at[2], up),
        remote(wh.at[first_half], wb.at[1, first_half], w_send.at[3], w_recv.at[3], down),
    ]
    for copy in w_copies:
        copy.start()
    def peer_of(step):
        return ((lo + step // 4) % 2) * 4 + (zz + step) % 4

    def heads_of_peer(step):
        return heads_of((lo + step // 4) % 2, (zz + step) % 4)

    def send_head(head, kinds=(0, 1, 2)):
        @pl.loop(1, PEERS)
        def _(step):
            peer = peer_of(step)
            columns = pl.ds(pl.multiple_of(heads_of_peer(step) + head * HD, HD), HD)
            for which in kinds:
                remote(
                    sources[which].at[0, :, columns],
                    targets[which].at[head, here, :],
                    qkv_send.at[which, head],
                    qkv_recv.at[which, head],
                    (f, peer),
                ).start()

    send_head(0)

    load_og.wait()
    load_gate.wait()
    gate = gv[pl.ds(step_ref[0], 1), :]
    for row in range(0, TOK, 32):
        rows = pl.ds(row, 32)
        sg[0, rows, :] = (gate * sg[0, rows, :].astype(F32)).astype(BF16)

    sg_across = remote(sg.at[0], sg.at[2], sg_send.at[1], sg_recv.at[1], across)
    sg_across.start()
    sg_mate = remote(sg.at[0], sg.at[1], sg_send.at[0], sg_recv.at[0], mate)
    sg_mate.start()

    load_xn = load(xn.at[0], xv)
    load_ef = load(ef, efv)
    load_ao = load(ao.at[0], av)
    load_mf = load(mixf, mfv)
    load_rf = load(resf, rfv)
    load_f = [
        load(
            mergedf.at[pl.ds(pl.multiple_of(kind * D + mine, HD), HPD * HD), :], fv.at[kind]
        )
        for kind in range(3)
    ]

    for head in range(HPD):
        for which in range(3):
            columns = pl.ds(pl.multiple_of(mine + head * HD, HD), HD)
            pltpu.make_async_copy(
                sources[which].at[0, :, columns],
                targets[which].at[head, here, :],
                qkv_recv.at[which, head],
            ).start()

    load_xn.wait()
    load_ef.wait()
    et[:, here] = dot(efv[...], xv[...], NT).astype(BF16)

    @pl.loop(1, PEERS)
    def _(step):
        peer = peer_of(step)
        remote(et.at[:, here], et.at[:, here], e_send, e_recv, (f, peer)).start()

    send_head(1)

    load_ao.wait()
    load_mf.wait()
    load_rf.wait()
    mixed_left = dot(mfv[...], av[...], NT)
    mixed_right = dot(sg[0], rfv[...])
    part[0] = dot(mixed_left, mixed_right, precision=lax.Precision.HIGHEST) * NORM

    def g_copies(place, image):
        chunk = (y + (0, 1, 3, 2)[place]) % 4
        token_block = s if image < 2 else s_across
        image_f = (f, mate[0], across_f, across_f + 1 - 2 * core)[image]
        peer = ((chunk + hi) % 2) * 4 + chunk
        columns = pl.ds(pl.multiple_of(token_block * TOK, TOK), TOK)
        target = gt.at[pl.ds(pl.multiple_of(core * WROWS, WROWS), WROWS), columns]
        source = gst.at[place, image]
        far = remote(source, target, g_send.at[place * 4 + image], g_recv, (image_f, peer))
        near = pltpu.make_async_copy(source, target, g_recv)
        return far, near, peer

    def make_g(first, last, image):
        weights = wb[first:last].reshape((last - first) * WROWS, D)
        grads = dot(weights, sg[image], NT).astype(BF16)
        for place in range(first, last):
            start = (place - first) * WROWS
            gst[place, image] = grads[start : start + WROWS]
            far, near, peer = g_copies(place, image)
            if image == 0:

                @pl.when(peer == s)
                def _():
                    near.start()

                @pl.when(peer != s)
                def _():
                    far.start()
            else:
                far.start()

    load_w.wait()
    make_g(0, 1, 0)
    sg_mate.wait_recv()
    make_g(0, 1, 1)
    w_copies[0].wait_recv()
    relay_up = remote(
        wb.at[2, first_half], wb.at[3, first_half], w_send.at[4], w_recv.at[4], up
    )
    relay_up.start()
    w_copies[1].wait_recv()
    relay_down = remote(
        wb.at[1, second_half], wb.at[3, second_half], w_send.at[5], w_recv.at[5], down
    )
    relay_down.start()

    def wait_head(head, kinds=(0, 1, 2)):
        for which in kinds:
            whole = targets[which].at[head]
            pltpu.make_async_copy(whole, whole, qkv_recv.at[which, head]).wait()

    def softmax_of(head, slot, with_values=True):
        softmax_head(
            head, slot, with_values, qb, kb_ref, vb, et, s_ref, p_ref, l_ref, o_ref, vt
        )

    rest = pl.ds(0, SEQ - TOK)
    pltpu.make_async_copy(et.at[:, rest], et.at[:, rest], e_recv).wait()
    wait_head(0)
    softmax_of(0, 0)
    w_copies[2].wait_recv()
    w_copies[3].wait_recv()


    make_g(1, 3, 0)
    make_g(1, 3, 1)
    sg_across.wait_recv()
    sg_pass = remote(sg.at[2], sg.at[3], sg_send.at[2], sg_recv.at[2], mate)
    sg_pass.start()
    make_g(0, 3, 2)
    relay_up.wait_recv()
    relay_down.wait_recv()
    for image in range(3):
        make_g(3, 4, image)
    sg_pass.wait_recv()
    make_g(0, 4, 3)
    send_head(2, (0, 1))
    send_head(2, (2,))
    wait_head(1)
    softmax_of(1, 1)

    for copy in load_f:
        copy.wait()
    pltpu.make_async_copy(gt, gt, g_recv).wait()
    part[1] = jnp.zeros((RIN, ROUT), F32)

    def gradients_of(head, slot):
        refs = (head, slot, qb, vb, gt, et, p_ref, l_ref, o_ref, accv, acck)
        gradient_block(0, True, *refs)

        @pl.loop(1, SEQ // GB)
        def _(block):
            gradient_block(pl.multiple_of(block * GB, GB), False, *refs)

        entry = et[...]
        value_part = accv[...]
        key_part = dot(entry, acck[:, :HD].astype(BF16))
        query_part = dot(acck[:, HD:].astype(BF16), kb_ref[head], TN)
        query_part = query_part[:RIN] + query_part[RIN:]
        columns = pl.ds(pl.multiple_of(head * HD, HD), HD)
        sketch = None
        for kind, piece in enumerate((query_part, key_part, value_part)):
            term = dot_split(piece, fv[kind, columns, :])
            sketch = term if sketch is None else sketch + term
        part[1] += sketch * NORM

    @pl.loop(0, 2)
    def _(head):
        gradients_of(head, head)

    wait_head(2, (0, 1))
    softmax_of(2, 0, False)
    wait_head(2, (2,))
    values_of_head(2, 0, vb, et, p_ref, o_ref, vt)
    gradients_of(2, 0)

    @pl.loop(1, PEERS)
    def _(step):
        peer = peer_of(step)
        rows = pl.ds(pl.multiple_of(peer * 8, 8), 8)
        remote(part.at[:, rows, :], gather.at[s], r_send, r_recv, (f, peer)).start()

    gather[s] = part[:, pl.ds(pl.multiple_of(s * 8, 8), 8), :]
    seven = gather.at[pl.ds(0, PEERS - 1)]
    pltpu.make_async_copy(seven, seven, r_recv).wait()
    summed = jnp.sum(gather[...], axis=0)
    for sketch in range(2):
        for row in range(8):
            out[0, sketch : sketch + 1, row * 128 : (row + 1) * 128] = summed[
                sketch, row : row + 1, :
            ]

    pltpu.make_async_copy(seven, seven, r_send).wait()
    pltpu.make_async_copy(et.at[:, rest], et.at[:, rest], e_send).wait()
    for head in range(HPD):
        for which in range(3):
            sent = targets[which].at[head, rest]
            pltpu.make_async_copy(sent, sent, qkv_send.at[which, head]).wait()
    for copy in w_copies + [relay_up, relay_down]:
        copy.wait_send()
    for copy in (sg_mate, sg_across, sg_pass):
        copy.wait_send()
    for image in range(4):
        for place in range(RINGS):
            far, _, peer = g_copies(place, image)
            if image == 0:
                pl.when(peer != s)(far.wait_send)
            else:
                far.wait_send()


def local(*operands):
    operands = list(operands)
    for place in (9, 11):
        operands[place] = operands[place].T
    dma = pltpu.SemaphoreType.DMA
    any_spec = pl.BlockSpec(memory_space=pl.ANY)
    in_specs = [any_spec] * 13
    in_specs[8] = pl.BlockSpec(memory_space=pltpu.SMEM)
    return pl.pallas_call(
        kernel,
        out_shape=jax.ShapeDtypeStruct((1, 2, RIN * ROUT // PEERS), F32),
        in_specs=in_specs,
        out_specs=pl.BlockSpec(memory_space=pltpu.VMEM),
        scratch_shapes=[
            pltpu.VMEM((HPD, SEQ, HD), BF16),
            pltpu.VMEM((HPD, SEQ, HD), BF16),
            pltpu.VMEM((HPD, SEQ, HD), BF16),
            pltpu.VMEM((HPD * HD, SEQ), BF16),
            pltpu.VMEM((RIN, SEQ), BF16),
            pltpu.VMEM((4, TOK, D), BF16),
            pltpu.VMEM((RINGS, WROWS, D), BF16),
            pltpu.VMEM((RINGS, 4, WROWS, TOK), BF16),
            pltpu.VMEM((TOK, D), BF16),
            pltpu.VMEM((TOK, D), BF16),
            pltpu.VMEM((64, D), F32),
            pltpu.VMEM((RIN, D), BF16),
            pltpu.VMEM((RIN, D), BF16),
            pltpu.VMEM((D, ROUT), BF16),
            pltpu.VMEM((3, HPD * HD, ROUT), BF16),
            pltpu.VMEM((2, SEQ, SB), F32),
            pltpu.VMEM((2, SEQ, SEQ), BF16),
            pltpu.VMEM((2, SEQ), F32),
            pltpu.VMEM((2, HD + RIN, SEQ), F32),
            pltpu.VMEM((HD + RIN, SEQ), BF16),
            pltpu.VMEM((RIN, HD), F32),
            pltpu.VMEM((SEQ, 2 * HD), F32),
            pltpu.VMEM((2, RIN, ROUT), F32),
            pltpu.VMEM((PEERS, 2, 8, ROUT), F32),
            dma((11,)),
            dma((3, HPD)),
            dma((3, HPD)),
            dma((6,)),
            dma((6,)),
            dma((3,)),
            dma((3,)),
            dma,
            dma((16,)),
            dma,
            dma,
            dma,
            dma,
        ],
        compiler_params=pltpu.CompilerParams(
            collective_id=0, has_side_effects=True, vmem_limit_bytes=60 << 20
        ),
        cost_estimate=pl.CostEstimate(
            flops=26 * 10**9, bytes_accessed=16 * 2**20, transcendentals=13 * 10**6
        ),
    )(*operands)


def solution(mesh):
    in_specs = (
        P("fsdp", "seq", None),
        P("fsdp", "seq", None),
        P("fsdp", "seq", None),
        P("fsdp", "seq", None),
        P("fsdp", "seq", None),
        P("fsdp", "seq", None),
        P("fsdp", None),
        P(),
        P("fsdp"),
        P(),
        P(),
        P(),
        P(),
    )
    out_specs = P("fsdp", None, "seq")
    return jax.shard_map(local, mesh=mesh, in_specs=in_specs, out_specs=out_specs, check_vma=False)
```
